512 devices in a mesh: dp: 32 (over y, x), mp: 16 (over z, core).
Axes of the slice: x: 4, y: 8, z: 8, core: 2. Of those that a mesh axis runs over, the one named last changes fastest.
Arguments:
- tokens: bfloat16 [4096, 4096], P('dp', 'mp'), may hold values from -6 to 6
- cotangent: bfloat16 [4096, 4096], P('dp', 'mp'), may hold values from -6 to 6
- block_mask: int32 [128, 32], P('mp'), may hold values from 0 to 1, as said below
- up_tiles: bfloat16 [512, 128, 128], P('mp'), may hold values from -0.25 to 0.25
- down_tiles: bfloat16 [512, 128, 128], P('mp'), may hold values from -0.25 to 0.25
Outputs:
- output: bfloat16 [4096, 4096], P('dp', 'mp')
- grad_tokens: bfloat16 [4096, 4096], P('dp', 'mp')
- grad_up: bfloat16 [512, 128, 128], P('mp')
- grad_down: bfloat16 [512, 128, 128], P('mp')
The draws below stay inside these ranges and needn't reach their ends.
Inputs may be any that keep to these rules, and one draw needn't show every extreme that they name: `block_mask`: entries are 0 or 1. Every row block has 2 or more active tiles; each group of 8 row blocks has at most 32 active tiles, some group exactly 32; groups g and g + 8 together hold exactly 48 active tiles.
All inputs are finite; a program needn't handle non-finite values.
Results may differ from the reference program's by a relative error of at most 0.02.
Values may be sent and summed in bfloat16 or wider, within the bound.
No kernel may reach another device: no remote copies, remote signals or barrier semaphores. Data moves between devices by JAX's collectives and lax.ppermute only.
A program may use at most 64 MiB of HBM per device.

```python
import jax
import jax.numpy as jnp
from jax import lax

D = 4096
BLK = 128
CB = 32
RB_DEV = 8
TCAP = 32
PAIR_CAP = 48
TOK_DEV = 128
TOKENS = 4096
N_DP = 32
N_MP = 16


def device_block(key, extras):
    key_units, key_cols = jax.random.split(key)
    unit_rows = jnp.repeat(jnp.arange(RB_DEV, dtype=jnp.int32), CB - 2)
    shuffled = jax.random.permutation(key_units, unit_rows)
    picked = (jnp.arange(unit_rows.shape[0], dtype=jnp.int32) < extras).astype(jnp.int32)
    hot_rows = (shuffled[:, None] == jnp.arange(RB_DEV, dtype=jnp.int32)[None, :]).astype(jnp.int32)
    counts = 2 + jnp.sum(hot_rows * picked[:, None], axis=0)
    scores = jax.random.randint(key_cols, (RB_DEV, CB), 0, 1 << 20) * CB + jnp.arange(CB, dtype=jnp.int32)[None, :]
    ranking = jnp.argsort(jnp.argsort(scores, axis=1), axis=1)
    return (ranking < counts[:, None]).astype(jnp.int32)


def draw_block_mask(key, part):
    key = jax.random.fold_in(key, 11)
    key_side, key_slack, key_exact, key_rows = jax.random.split(key, 4)
    half_count = N_MP // 2
    heavy_side = jax.random.randint(key_side, (half_count,), 0, 2)
    slack_tiles = jax.random.randint(key_slack, (half_count,), 0, 5)
    exact_pair = jax.random.randint(key_exact, (), 0, half_count)
    slack_tiles = jnp.where(jnp.arange(half_count) == exact_pair, 0, slack_tiles)
    heavy_total = TCAP - slack_tiles
    light_total = PAIR_CAP - heavy_total
    first_total = jnp.where(heavy_side == 1, heavy_total, light_total)
    second_total = PAIR_CAP - first_total
    device_totals = jnp.concatenate([first_total, second_total]).astype(jnp.int32)
    device_keys = jax.random.split(key_rows, N_MP)
    blocks = jax.vmap(device_block)(device_keys, device_totals - 2 * RB_DEV)
    return blocks.reshape(N_MP * RB_DEV, CB).astype(jnp.int32)


def shard_levels(rng, dims, pieces, low, largest):
    def one(dim, blocks):
        steps = jax.random.uniform(jax.random.fold_in(jax.random.fold_in(rng, 6), dim), (blocks,), jnp.float32, low / len(pieces), largest / len(pieces))
        return jnp.repeat(jnp.exp(steps), dims[dim] // blocks).reshape((-1,) + (1,) * (len(dims) - dim - 1))

    loudness = one(*pieces[0])
    for cut in pieces[1:]:
        loudness = loudness * one(*cut)
    return loudness


def scatter_about(key, dims, spread, bound, shards=(), kind=jnp.bfloat16):
    values = spread * jax.random.normal(key, dims, jnp.float32)
    if shards:
        values = values * shard_levels(key, dims, shards, -0.22, 0.18)
    return jnp.clip(values, -bound, bound).astype(kind)


def setup_inputs(seed: int = 0) -> dict:
    key_of = jax.random.split(jax.random.key(seed), 6)
    tokens = scatter_about(key_of[0], (TOKENS, D), 1.0, 6.0, ((0, 32), (1, 16)))
    cotangent = scatter_about(key_of[1], (TOKENS, D), 1.0, 6.0, ((0, 32), (1, 16)))
    block_mask = draw_block_mask(jax.random.fold_in(key_of[5], 71), 0)
    up_tiles = scatter_about(key_of[3], (N_MP * TCAP, BLK, BLK), (4 * BLK) ** -0.5, 0.25, ((0, 16),))
    down_tiles = scatter_about(key_of[4], (N_MP * TCAP, BLK, BLK), (4 * BLK) ** -0.5, 0.25, ((0, 16),))
    return {"tokens": tokens, "cotangent": cotangent, "block_mask": block_mask, "up_tiles": up_tiles, "down_tiles": down_tiles}


def gelu_value(hidden):
    argument = 0.7978845608 * (hidden + 0.044715 * hidden * hidden * hidden)
    return 0.5 * hidden * (1.0 + jnp.tanh(argument))


def gelu_slope(hidden):
    argument = 0.7978845608 * (hidden + 0.044715 * hidden * hidden * hidden)
    tangent = jnp.tanh(argument)
    inner_slope = 0.7978845608 * (1.0 + 3.0 * 0.044715 * hidden * hidden)
    return 0.5 * (1.0 + tangent) + 0.5 * hidden * (1.0 - tangent * tangent) * inner_slope


def round_trip(value):
    return lax.optimization_barrier(value.astype(jnp.bfloat16)).astype(jnp.float32)


def slot_table(local_mask, capacity):
    flattened = local_mask.reshape(-1).astype(jnp.int32)
    position = jnp.cumsum(flattened).astype(jnp.int32) - 1
    slot_ids = jnp.arange(capacity, dtype=jnp.int32)
    cell_ids = jnp.arange(flattened.shape[0], dtype=jnp.int32)
    matches = (flattened[None, :] == 1) & (position[None, :] == slot_ids[:, None])
    chosen = jnp.sum(jnp.where(matches, cell_ids[None, :], 0), axis=1).astype(jnp.int32)
    in_use = slot_ids < jnp.sum(flattened).astype(jnp.int32)
    col_count = local_mask.shape[1]
    return chosen // col_count, chosen % col_count, in_use


def reference(tokens, cotangent, block_mask, up_tiles, down_tiles):
    token_count = tokens.shape[0]
    panels_in = tokens.reshape(token_count, CB, BLK).astype(jnp.float32)
    panels_back = cotangent.reshape(token_count, CB, BLK).astype(jnp.float32)
    group_masks = block_mask.reshape(N_MP, RB_DEV, CB)
    group_up = up_tiles.reshape(N_MP, TCAP, BLK, BLK)
    group_down = down_tiles.reshape(N_MP, TCAP, BLK, BLK)

    def device_step(running, group_data):
        out_total, grad_total = running
        local_mask, up_local, down_local = group_data
        slot_rows, slot_cols, in_use = slot_table(local_mask, TCAP)
        weight_use = in_use.astype(jnp.float32)
        row_hot = (slot_rows[:, None] == jnp.arange(RB_DEV, dtype=jnp.int32)[None, :]).astype(jnp.float32) * weight_use[:, None]
        column_hot = (slot_cols[:, None] == jnp.arange(CB, dtype=jnp.int32)[None, :]).astype(jnp.float32) * weight_use[:, None]
        up_float = up_local.astype(jnp.float32)
        down_float = down_local.astype(jnp.float32)
        in_picked = jnp.take(panels_in, slot_cols, axis=1)
        back_picked = jnp.take(panels_back, slot_cols, axis=1)
        hidden_part = jnp.einsum("tsi,sio->tso", in_picked, up_float)
        dact_part = jnp.einsum("tsc,shc->tsh", back_picked, down_float)
        hidden = jnp.einsum("tso,sr->tro", hidden_part, row_hot)
        dact = jnp.einsum("tsh,sr->trh", dact_part, row_hot)
        activated = gelu_value(hidden).astype(jnp.bfloat16)
        pre_grad = (dact * gelu_slope(hidden)).astype(jnp.bfloat16)
        act_picked = jnp.take(activated, slot_rows, axis=1).astype(jnp.float32)
        pre_picked = jnp.take(pre_grad, slot_rows, axis=1).astype(jnp.float32)
        out_part = jnp.einsum("tsh,shc->tsc", act_picked, down_float)
        out_cols = jnp.einsum("tsc,sk->tkc", out_part, column_hot)
        grad_part = jnp.einsum("tsh,sih->tsi", pre_picked, up_float)
        grad_cols = jnp.einsum("tsc,sk->tkc", grad_part, column_hot)
        out_total = out_total + round_trip(out_cols)
        grad_total = grad_total + round_trip(grad_cols)
        act_group = act_picked.reshape(N_DP, TOK_DEV, TCAP, BLK)
        back_group = back_picked.reshape(N_DP, TOK_DEV, TCAP, BLK)
        in_group = in_picked.reshape(N_DP, TOK_DEV, TCAP, BLK)
        pre_group = pre_picked.reshape(N_DP, TOK_DEV, TCAP, BLK)
        down_shards = jnp.einsum("gtsh,gtsc->gshc", act_group, back_group)
        up_shards = jnp.einsum("gtsi,gtsh->gsih", in_group, pre_group)
        down_grad = (jnp.sum(round_trip(down_shards), axis=0) * weight_use[:, None, None]).astype(jnp.bfloat16)
        up_grad = (jnp.sum(round_trip(up_shards), axis=0) * weight_use[:, None, None]).astype(jnp.bfloat16)
        return (out_total, grad_total), (up_grad, down_grad)

    start = (jnp.zeros((token_count, CB, BLK), jnp.float32), jnp.zeros((token_count, CB, BLK), jnp.float32))
    finals, stacked = lax.scan(device_step, start, (group_masks, group_up, group_down))
    output = finals[0].reshape(token_count, CB * BLK).astype(jnp.bfloat16)
    grad_tokens = finals[1].reshape(token_count, CB * BLK).astype(jnp.bfloat16)
    grad_up = stacked[0].reshape(N_MP * TCAP, BLK, BLK)
    grad_down = stacked[1].reshape(N_MP * TCAP, BLK, BLK)
    return (output, grad_tokens, grad_up, grad_down)
```

```python
import jax
import jax.numpy as jnp
from jax import lax
from jax.experimental import pallas as pl
from jax.experimental.pallas import tpu as pltpu
from jax.sharding import PartitionSpec as P

BF = jnp.bfloat16
F32 = jnp.float32
VM = pltpu.CompilerParams(vmem_limit_bytes=48 * 1024 * 1024)
NX, NY, NZ = 4, 8, 8
X_GROUPS = [[NX * y + x for x in range(NX)] for y in range(NY)]
Y_GROUPS = [[NX * y + x for y in range(NY)] for x in range(NX)]
Z_GROUPS = [[2 * z + c for z in range(NZ)] for c in range(2)]
CORE_SWAP = [(i, i ^ 1) for i in range(2 * NZ)]
SLOTS, ROWS, COLS, BLK = 32, 8, 32, 128


def gelu_pair(hidden, dact):
    inner = 0.7978845608 * (hidden + 0.044715 * hidden * hidden * hidden)
    tangent = jnp.tanh(inner)
    inner_slope = 0.7978845608 * (1.0 + 3.0 * 0.044715 * hidden * hidden)
    value = 0.5 * hidden * (1.0 + tangent)
    slope = 0.5 * (1.0 + tangent) + 0.5 * hidden * (1.0 - tangent * tangent) * inner_slope
    return value.astype(BF), (dact * slope).astype(BF)


def nn(a, b):
    return lax.dot_general(a, b, (((1,), (0,)), ((), ())), preferred_element_type=F32)


def nt(a, b):
    return lax.dot_general(a, b, (((1,), (1,)), ((), ())), preferred_element_type=F32)


def prep_kernel(tok_ref, cot_ref, out_ref):
    for j in range(2):
        tok_t = tok_ref[:, j * BLK : (j + 1) * BLK].T
        cot = cot_ref[:, j * BLK : (j + 1) * BLK]
        for z in range(NZ):
            out_ref[z, j] = tok_t
            out_ref[z, 2 + j] = cot


def table_kernel(mask_ref, out_ref, cells):
    count = jnp.int32(0)
    for cell in range(ROWS * COLS):
        cells[count] = jnp.int32(cell)
        count = count + mask_ref[cell // COLS, cell % COLS]
    last_row = jnp.int32(-1)
    for s in range(SLOTS):
        used = jnp.int32(s) < count
        cell = jnp.where(used, cells[s], ROWS * COLS - 1)
        row = cell >> 5
        out_ref[s] = cell & 31
        out_ref[SLOTS + s] = row
        out_ref[2 * SLOTS + s] = jnp.where(row == last_row, 0, 1)
        out_ref[3 * SLOTS + s] = jnp.where(used, 1, 0)
        last_row = row


def weights_kernel(up_ref, down_ref, up_t_ref, down_t_ref):
    for s in range(SLOTS):
        up_t_ref[s] = up_ref[s].T
        down_t_ref[s] = down_ref[s].T


def first_kernel(
    table_ref, core_ref, own_ref, other_ref, up_t_ref, down_ref, grads_ref, act_ref, pre_ref, panels, hid, dac
):
    core = core_ref[0]
    panels[0] = own_ref[...]
    panels[1] = other_ref[...]

    def place(s):
        col = table_ref[s]
        return ((col >> 1) & 1) ^ core, col >> 2, col & 1

    hid_sum = jnp.zeros((BLK, BLK), F32)
    dac_sum = jnp.zeros((BLK, BLK), F32)
    for s in range(SLOTS):
        side, z, j = place(s)
        row = table_ref[SLOTS + s]
        fresh = table_ref[2 * SLOTS + s] == 1
        used = table_ref[3 * SLOTS + s] == 1
        hid_part = nn(up_t_ref[s], panels[side, z, j])
        dac_part = nt(down_ref[s], panels[side, z, 2 + j])
        hid_sum = jnp.where(fresh, 0.0, hid_sum) + jnp.where(used, hid_part, 0.0)
        dac_sum = jnp.where(fresh, 0.0, dac_sum) + jnp.where(used, dac_part, 0.0)
        hid[row] = hid_sum
        dac[row] = dac_sum
    for r in range(ROWS):
        act, pre = gelu_pair(hid[r], dac[r])
        act_ref[r] = act
        pre_ref[r] = pre
    for s in range(SLOTS):
        side, z, j = place(s)
        row = table_ref[SLOTS + s]
        used = table_ref[3 * SLOTS + s] == 1
        up_part = nt(panels[side, z, j], pre_ref[row])
        down_part = nn(act_ref[row], panels[side, z, 2 + j])
        grads_ref[s // 8, 0, s % 8] = jnp.where(used, up_part, 0.0).astype(BF)
        grads_ref[s // 8, 1, s % 8] = jnp.where(used, down_part, 0.0).astype(BF)


def second_kernel(table_ref, core_ref, act_ref, pre_ref, down_t_ref, up_ref, own_ref, send_ref, out_sum, grad_sum):
    core = core_ref[0]
    out_sum[...] = jnp.zeros_like(out_sum)
    grad_sum[...] = jnp.zeros_like(grad_sum)
    for s in range(SLOTS):
        col = table_ref[s]
        row = table_ref[SLOTS + s]
        used = table_ref[3 * SLOTS + s] == 1
        out_part = nn(down_t_ref[s], act_ref[row])
        grad_part = nn(up_ref[s], pre_ref[row])
        out_sum[col] += jnp.where(used, out_part, 0.0)
        grad_sum[col] += jnp.where(used, grad_part, 0.0)
    for z in range(NZ):
        for j in range(2):
            own = 4 * z + 2 * core + j
            other = 4 * z + 2 * (1 - core) + j
            own_ref[z, j] = out_sum[own].astype(BF)
            own_ref[z, 2 + j] = grad_sum[own].astype(BF)
            send_ref[z, j] = out_sum[other].astype(BF)
            send_ref[z, 2 + j] = grad_sum[other].astype(BF)


def add_kernel(a_ref, b_ref, out_ref):
    out_ref[...] = (a_ref[...].astype(F32) + b_ref[...].astype(F32)).astype(BF)


def x_sum_kernel(in_ref, out_ref):
    for y in range(NY):
        for k in range(2):
            total = in_ref[0, k, y].astype(F32)
            for x in range(1, NX):
                total = total + in_ref[x, k, y].astype(F32)
            out_ref[y, k] = total.astype(BF)


def y_sum_kernel(in_ref, out_ref):
    for k in range(2):
        total = in_ref[0, k].astype(F32)
        for y in range(1, NY):
            total = total + in_ref[y, k].astype(F32)
        total = total.astype(BF)
        for y in range(NY):
            out_ref[y, k] = total


def spread_kernel(in_ref, out_ref):
    for y in range(NY):
        for k in range(2):
            tile = in_ref[y, k]
            for x in range(NX):
                out_ref[x, k, y] = tile


def split_kernel(in_ref, up_ref, down_ref):
    for x in range(NX):
        up_ref[x * 8 : (x + 1) * 8] = in_ref[x, 0]
        down_ref[x * 8 : (x + 1) * 8] = in_ref[x, 1]


def final_kernel(in_ref, out_ref, grad_ref):
    for j in range(2):
        out_ref[:, j * BLK : (j + 1) * BLK] = in_ref[j].T
        grad_ref[:, j * BLK : (j + 1) * BLK] = in_ref[2 + j].T


def whole(count):
    return [pl.BlockSpec(memory_space=pltpu.VMEM)] * count


def smem(count):
    return [pl.BlockSpec(memory_space=pltpu.SMEM)] * count


def shape(*dims, dtype=BF):
    return jax.ShapeDtypeStruct(dims, dtype)


def call(kernel, outs, operands, n_smem=0, scratch=(), flops=0, moved=0, out_smem=False):
    many = isinstance(outs, (list, tuple))
    n_out = len(outs) if many else 1
    out_specs = smem(n_out) if out_smem else whole(n_out)
    return pl.pallas_call(
        kernel,
        out_shape=outs,
        in_specs=smem(n_smem) + whole(len(operands) - n_smem),
        out_specs=out_specs if many else out_specs[0],
        scratch_shapes=list(scratch),
        compiler_params=VM,
        cost_estimate=pl.CostEstimate(flops=flops, bytes_accessed=moved, transcendentals=0),
    )(*operands)


def exchange(x, axis, groups):
    return lax.all_to_all(x, axis, 0, 0, tiled=True, axis_index_groups=groups)


def body(tokens, cotangent, block_mask, up_tiles, down_tiles):
    mib = 1 << 20
    core = (lax.axis_index("mp") % 2).astype(jnp.int32).reshape(1)
    sent = call(prep_kernel, shape(NZ, 4, BLK, BLK), (tokens, cotangent), moved=mib)
    own_panels = exchange(sent, "mp", Z_GROUPS)
    table = call(
        table_kernel,
        shape(4 * SLOTS, dtype=jnp.int32),
        (block_mask,),
        n_smem=1,
        scratch=[pltpu.SMEM((ROWS * COLS + 8,), jnp.int32)],
        out_smem=True,
        flops=mib,
        moved=1024,
    )
    up_t, down_t = call(
        weights_kernel,
        [shape(SLOTS, BLK, BLK), shape(SLOTS, BLK, BLK)],
        (up_tiles, down_tiles),
        moved=4 * mib,
    )
    other_panels = lax.ppermute(own_panels, "mp", CORE_SWAP)
    product = 2 * SLOTS * BLK * BLK * BLK
    grads, act, pre = call(
        first_kernel,
        [shape(NX, 2, 8, BLK, BLK), shape(ROWS, BLK, BLK), shape(ROWS, BLK, BLK)],
        (table, core, own_panels, other_panels, up_t, down_tiles),
        n_smem=2,
        scratch=[
            pltpu.VMEM((2, NZ, 4, BLK, BLK), BF),
            pltpu.VMEM((ROWS, BLK, BLK), F32),
            pltpu.VMEM((ROWS, BLK, BLK), F32),
        ],
        flops=4 * product,
        moved=6 * mib,
    )
    own_part, other_part = call(
        second_kernel,
        [shape(NZ, 4, BLK, BLK), shape(NZ, 4, BLK, BLK)],
        (table, core, act, pre, down_t, up_tiles),
        n_smem=2,
        scratch=[pltpu.VMEM((COLS, BLK, BLK), F32), pltpu.VMEM((COLS, BLK, BLK), F32)],
        flops=2 * product,
        moved=5 * mib,
    )
    from_other = lax.ppermute(other_part, "mp", CORE_SWAP)
    chip_part = call(add_kernel, shape(NZ, 4, BLK, BLK), (own_part, from_other), moved=3 * mib)
    by_x = exchange(grads, "dp", X_GROUPS)
    x_done = call(x_sum_kernel, shape(NY, 2, BLK, BLK), (by_x,), moved=3 * mib)
    x_done, chip_part = lax.optimization_barrier((x_done, chip_part))
    columns = lax.psum_scatter(
        chip_part.reshape(NZ * 4, BLK, BLK), "mp", scatter_dimension=0, axis_index_groups=Z_GROUPS, tiled=True
    )
    output, grad_tokens = call(
        final_kernel, [shape(BLK, 2 * BLK), shape(BLK, 2 * BLK)], (columns,), moved=mib // 4
    )
    by_y = exchange(x_done, "dp", Y_GROUPS)
    y_done = call(y_sum_kernel, shape(NY, 2, BLK, BLK), (by_y,), moved=mib)
    all_y = exchange(y_done, "dp", Y_GROUPS)
    spread = call(spread_kernel, shape(NX, 2, NY, BLK, BLK), (all_y,), moved=3 * mib)
    all_x = exchange(spread, "dp", X_GROUPS)
    grad_up, grad_down = call(
        split_kernel, [shape(SLOTS, BLK, BLK), shape(SLOTS, BLK, BLK)], (all_x,), moved=4 * mib
    )
    return output, grad_tokens, grad_up, grad_down


def solution(mesh):
    in_specs = (
        P("dp", "mp"),
        P("dp", "mp"),
        P("mp", None),
        P("mp", None, None),
        P("mp", None, None),
    )
    out_specs = (P("dp", "mp"), P("dp", "mp"), P("mp", None, None), P("mp", None, None))
    return jax.shard_map(body, mesh=mesh, in_specs=in_specs, out_specs=out_specs, check_vma=False)
```

```python
import jax
import jax.numpy as jnp
from jax import lax
from jax.experimental import pallas as pl
from jax.experimental.pallas import tpu as pltpu
from jax.sharding import PartitionSpec as P

BF = jnp.bfloat16
F32 = jnp.float32
VM = pltpu.CompilerParams(vmem_limit_bytes=48 * 1024 * 1024)
NX, NY, NZ = 4, 8, 8
X_GROUPS = [[NX * y + x for x in range(NX)] for y in range(NY)]
Y_GROUPS = [[NX * y + x for y in range(NY)] for x in range(NX)]
Z_GROUPS = [[2 * z + c for z in range(NZ)] for c in range(2)]
CORE_SWAP = [(i, i ^ 1) for i in range(2 * NZ)]
PAIR_SWAP = [(i, i ^ 2) for i in range(2 * NZ)]
SLOTS, ROWS, COLS, BLK = 32, 8, 32, 128


def gelu_pair(hidden, dact):
    inner = 0.7978845608 * (hidden + 0.044715 * hidden * hidden * hidden)
    tangent = jnp.tanh(inner)
    inner_slope = 0.7978845608 * (1.0 + 3.0 * 0.044715 * hidden * hidden)
    value = 0.5 * hidden * (1.0 + tangent)
    slope = 0.5 * (1.0 + tangent) + 0.5 * hidden * (1.0 - tangent * tangent) * inner_slope
    return value.astype(BF), (dact * slope).astype(BF)


def nn(a, b):
    return lax.dot_general(a, b, (((1,), (0,)), ((), ())), preferred_element_type=F32)


def nt(a, b):
    return lax.dot_general(a, b, (((1,), (1,)), ((), ())), preferred_element_type=F32)


def prep_kernel(tok_ref, cot_ref, out_ref):
    for j in range(2):
        tok_t = tok_ref[:, j * BLK : (j + 1) * BLK].T
        cot = cot_ref[:, j * BLK : (j + 1) * BLK]
        for z in range(NZ):
            out_ref[z, j] = tok_t
            out_ref[z, 2 + j] = cot


def table_kernel(mask_ref, out_ref, cells):
    count = jnp.int32(0)
    for cell in range(ROWS * COLS):
        cells[count] = jnp.int32(cell)
        count = count + mask_ref[cell // COLS, cell % COLS]
    last_row = jnp.int32(-1)
    for s in range(SLOTS):
        used = jnp.int32(s) < count
        cell = jnp.where(used, cells[s], ROWS * COLS - 1)
        row = cell >> 5
        out_ref[s] = cell & 31
        out_ref[SLOTS + s] = row
        out_ref[2 * SLOTS + s] = jnp.where(row == last_row, 0, 1)
        out_ref[3 * SLOTS + s] = jnp.where(used, 1, 0)
        last_row = row


def weights_kernel(up_ref, down_ref, up_t_ref, down_t_ref):
    for s in range(SLOTS):
        up_t_ref[s] = up_ref[s].T
        down_t_ref[s] = down_ref[s].T


def first_kernel(
    table_ref, place_ref, own_ref, other_ref, up_t_ref, down_ref, grads_ref, act_ref, pre_ref, panels, hid, dac
):
    core = place_ref[0]
    panels[0] = own_ref[...]
    panels[1] = other_ref[...]

    def place(s):
        col = table_ref[s]
        return ((col >> 1) & 1) ^ core, col >> 2, col & 1

    hid_sum = jnp.zeros((BLK, BLK), F32)
    dac_sum = jnp.zeros((BLK, BLK), F32)
    for s in range(SLOTS):
        side, z, j = place(s)
        row = table_ref[SLOTS + s]
        fresh = table_ref[2 * SLOTS + s] == 1
        used = table_ref[3 * SLOTS + s] == 1
        hid_part = nn(up_t_ref[s], panels[side, z, j])
        dac_part = nt(down_ref[s], panels[side, z, 2 + j])
        hid_sum = jnp.where(fresh, 0.0, hid_sum) + jnp.where(used, hid_part, 0.0)
        dac_sum = jnp.where(fresh, 0.0, dac_sum) + jnp.where(used, dac_part, 0.0)
        hid[row] = hid_sum
        dac[row] = dac_sum
    for r in range(ROWS):
        act, pre = gelu_pair(hid[r], dac[r])
        act_ref[r] = act
        pre_ref[r] = pre
    for s in range(SLOTS):
        side, z, j = place(s)
        row = table_ref[SLOTS + s]
        used = table_ref[3 * SLOTS + s] == 1
        up_part = nt(panels[side, z, j], pre_ref[row])
        down_part = nn(act_ref[row], panels[side, z, 2 + j])
        grads_ref[s // 8, 0, s % 8] = jnp.where(used, up_part, 0.0).astype(BF)
        grads_ref[s // 8, 1, s % 8] = jnp.where(used, down_part, 0.0).astype(BF)


def second_kernel(table_ref, place_ref, act_ref, pre_ref, down_t_ref, up_ref, own_ref, send_ref, out_sum, grad_sum):
    core = place_ref[0]
    out_sum[...] = jnp.zeros_like(out_sum)
    grad_sum[...] = jnp.zeros_like(grad_sum)
    for s in range(SLOTS):
        col = table_ref[s]
        row = table_ref[SLOTS + s]
        used = table_ref[3 * SLOTS + s] == 1
        out_part = nn(down_t_ref[s], act_ref[row])
        grad_part = nn(up_ref[s], pre_ref[row])
        out_sum[col] += jnp.where(used, out_part, 0.0)
        grad_sum[col] += jnp.where(used, grad_part, 0.0)
    for z in range(NZ):
        for j in range(2):
            own = 4 * z + 2 * core + j
            other = 4 * z + 2 * (1 - core) + j
            own_ref[z, j] = out_sum[own].astype(BF)
            own_ref[z, 2 + j] = grad_sum[own].astype(BF)
            send_ref[z, j] = out_sum[other].astype(BF)
            send_ref[z, 2 + j] = grad_sum[other].astype(BF)


def chip_add_kernel(place_ref, a_ref, b_ref, keep_ref, send_ref):
    odd = place_ref[1] & 1
    for half in range(NZ // 2):
        near = 2 * half + odd
        far = 2 * half + 1 - odd
        keep_ref[half] = (a_ref[near].astype(F32) + b_ref[near].astype(F32)).astype(BF)
        send_ref[half] = (a_ref[far].astype(F32) + b_ref[far].astype(F32)).astype(BF)


def pair_add_kernel(place_ref, a_ref, b_ref, *out_refs):
    mine = place_ref[1] >> 1
    for hop in range(NZ // 2):
        there = (mine + hop) & (NZ // 2 - 1)
        out_refs[hop][...] = (a_ref[there].astype(F32) + b_ref[there].astype(F32)).astype(BF)


def x_sum_kernel(in_ref, out_ref):
    for y in range(NY):
        for k in range(2):
            total = in_ref[0, k, y].astype(F32)
            for x in range(1, NX):
                total = total + in_ref[x, k, y].astype(F32)
            out_ref[y, k] = total.astype(BF)


def y_sum_kernel(in_ref, out_ref):
    for k in range(2):
        total = in_ref[0, k].astype(F32)
        for y in range(1, NY):
            total = total + in_ref[y, k].astype(F32)
        total = total.astype(BF)
        for y in range(NY):
            out_ref[y, k] = total


def spread_kernel(in_ref, out_ref):
    for y in range(NY):
        for k in range(2):
            tile = in_ref[y, k]
            for x in range(NX):
                out_ref[x, k, y] = tile


def split_kernel(in_ref, up_ref, down_ref):
    for x in range(NX):
        up_ref[x * 8 : (x + 1) * 8] = in_ref[x, 0]
        down_ref[x * 8 : (x + 1) * 8] = in_ref[x, 1]


def final_kernel(*refs):
    in_refs, out_ref, grad_ref = refs[:-2], refs[-2], refs[-1]
    for j in range(4):
        total = in_refs[0][j].astype(F32)
        for in_ref in in_refs[1:]:
            total = total + in_ref[j].astype(F32)
        goal = out_ref if j < 2 else grad_ref
        goal[:, (j % 2) * BLK : (j % 2 + 1) * BLK] = total.T.astype(BF)


def whole(count):
    return [pl.BlockSpec(memory_space=pltpu.VMEM)] * count


def smem(count):
    return [pl.BlockSpec(memory_space=pltpu.SMEM)] * count


def shape(*dims, dtype=BF):
    return jax.ShapeDtypeStruct(dims, dtype)


def call(kernel, outs, operands, n_smem=0, scratch=(), flops=0, moved=0, out_smem=False):
    many = isinstance(outs, (list, tuple))
    n_out = len(outs) if many else 1
    out_specs = smem(n_out) if out_smem else whole(n_out)
    return pl.pallas_call(
        kernel,
        out_shape=outs,
        in_specs=smem(n_smem) + whole(len(operands) - n_smem),
        out_specs=out_specs if many else out_specs[0],
        scratch_shapes=list(scratch),
        compiler_params=VM,
        cost_estimate=pl.CostEstimate(flops=flops, bytes_accessed=moved, transcendentals=0),
    )(*operands)


def exchange(x, axis, groups):
    return lax.all_to_all(x, axis, 0, 0, tiled=True, axis_index_groups=groups)


def body(tokens, cotangent, block_mask, up_tiles, down_tiles):
    mib = 1 << 20
    position = lax.axis_index("mp")
    place = jnp.stack([position & 1, position >> 1]).astype(jnp.int32)
    sent = call(prep_kernel, shape(NZ, 4, BLK, BLK), (tokens, cotangent), moved=mib)
    own_panels = exchange(sent, "mp", Z_GROUPS)
    table = call(
        table_kernel,
        shape(4 * SLOTS, dtype=jnp.int32),
        (block_mask,),
        n_smem=1,
        scratch=[pltpu.SMEM((ROWS * COLS + 8,), jnp.int32)],
        out_smem=True,
        flops=mib,
        moved=1024,
    )
    up_t, down_t = call(
        weights_kernel,
        [shape(SLOTS, BLK, BLK), shape(SLOTS, BLK, BLK)],
        (up_tiles, down_tiles),
        moved=4 * mib,
    )
    other_panels = lax.ppermute(own_panels, "mp", CORE_SWAP)
    product = 2 * SLOTS * BLK * BLK * BLK
    grads, act, pre = call(
        first_kernel,
        [shape(NX, 2, 8, BLK, BLK), shape(ROWS, BLK, BLK), shape(ROWS, BLK, BLK)],
        (table, place, own_panels, other_panels, up_t, down_tiles),
        n_smem=2,
        scratch=[
            pltpu.VMEM((2, NZ, 4, BLK, BLK), BF),
            pltpu.VMEM((ROWS, BLK, BLK), F32),
            pltpu.VMEM((ROWS, BLK, BLK), F32),
        ],
        flops=4 * product,
        moved=6 * mib,
    )
    own_part, other_part = call(
        second_kernel,
        [shape(NZ, 4, BLK, BLK), shape(NZ, 4, BLK, BLK)],
        (table, place, act, pre, down_t, up_tiles),
        n_smem=2,
        scratch=[pltpu.VMEM((COLS, BLK, BLK), F32), pltpu.VMEM((COLS, BLK, BLK), F32)],
        flops=2 * product,
        moved=5 * mib,
    )
    from_other = lax.ppermute(other_part, "mp", CORE_SWAP)
    chip_keep, chip_send = call(
        chip_add_kernel,
        [shape(NZ // 2, 4, BLK, BLK)] * 2,
        (place, own_part, from_other),
        n_smem=1,
        moved=3 * mib,
    )
    by_x = exchange(grads, "dp", X_GROUPS)
    by_x, chip_keep, chip_send = lax.optimization_barrier((by_x, chip_keep, chip_send))
    from_pair = lax.ppermute(chip_send, "mp", PAIR_SWAP)
    x_done = call(x_sum_kernel, shape(NY, 2, BLK, BLK), (by_x,), moved=3 * mib)
    by_y = exchange(x_done, "dp", Y_GROUPS)
    hops = call(
        pair_add_kernel,
        [shape(4, BLK, BLK)] * (NZ // 2),
        (place, chip_keep, from_pair),
        n_smem=1,
        moved=3 * mib // 2,
    )
    by_y, hops = lax.optimization_barrier((by_y, hops))
    columns = [hops[0]]
    for hop in range(1, NZ // 2):
        pairs = [(2 * z + c, 2 * ((z + 2 * hop) % NZ) + c) for z in range(NZ) for c in range(2)]
        columns.append(lax.ppermute(hops[hop], "mp", pairs))
    y_done = call(y_sum_kernel, shape(NY, 2, BLK, BLK), (by_y,), moved=mib)
    all_y = exchange(y_done, "dp", Y_GROUPS)
    output, grad_tokens = call(
        final_kernel, [shape(BLK, 2 * BLK), shape(BLK, 2 * BLK)], columns, moved=mib
    )
    spread = call(spread_kernel, shape(NX, 2, NY, BLK, BLK), (all_y,), moved=3 * mib)
    all_x = exchange(spread, "dp", X_GROUPS)
    grad_up, grad_down = call(
        split_kernel, [shape(SLOTS, BLK, BLK), shape(SLOTS, BLK, BLK)], (all_x,), moved=4 * mib
    )
    return output, grad_tokens, grad_up, grad_down


def solution(mesh):
    in_specs = (
        P("dp", "mp"),
        P("dp", "mp"),
        P("mp", None),
        P("mp", None, None),
        P("mp", None, None),
    )
    out_specs = (P("dp", "mp"), P("dp", "mp"), P("mp", None, None), P("mp", None, None))
    return jax.shard_map(body, mesh=mesh, in_specs=in_specs, out_specs=out_specs, check_vma=False)
```

```python
import functools

import jax
import jax.numpy as jnp
from jax import lax
from jax.experimental import pallas as pl
from jax.experimental.pallas import tpu as pltpu
from jax.sharding import PartitionSpec as P

BF = jnp.bfloat16
F32 = jnp.float32
VM = pltpu.CompilerParams(vmem_limit_bytes=48 * 1024 * 1024)
NX, NY, NZ = 4, 8, 8
N_MP = 2 * NZ


def flat(x, y, mp):
    return ((y % NY) * NX + x % NX) * N_MP + mp


NEAR_GROUPS = [
    [flat(2 * bx + mp % 2 + i, 2 * by + mp % 2 + j, mp) for j in range(2) for i in range(2)]
    for mp in range(N_MP)
    for by in range(NY // 2)
    for bx in range(NX // 2)
]
FAR_GROUPS = [
    [flat(2 * bx + mp % 2 + i, 2 * by + mp % 2 + j, mp) for by in range(NY // 2) for bx in range(NX // 2)]
    for mp in range(N_MP)
    for j in range(2)
    for i in range(2)
]
Z_GROUPS = [[2 * z + c for z in range(NZ)] for c in range(2)]
CORE_SWAP = [(i, i ^ 1) for i in range(2 * NZ)]


def z_swap(level):
    step = 1 << level
    return [
        (2 * z + c, 2 * ((z + (step if ((z >> level) + c) % 2 == 0 else -step)) % NZ) + c)
        for z in range(NZ)
        for c in range(2)
    ]


SLOTS, ROWS, COLS, BLK = 32, 8, 32, 128


def gelu_pair(hidden, dact):
    inner = 0.7978845608 * (hidden + 0.044715 * hidden * hidden * hidden)
    tangent = jnp.tanh(inner)
    inner_slope = 0.7978845608 * (1.0 + 3.0 * 0.044715 * hidden * hidden)
    value = 0.5 * hidden * (1.0 + tangent)
    slope = 0.5 * (1.0 + tangent) + 0.5 * hidden * (1.0 - tangent * tangent) * inner_slope
    return value.astype(BF), (dact * slope).astype(BF)


def nn(a, b):
    return lax.dot_general(a, b, (((1,), (0,)), ((), ())), preferred_element_type=F32)


def nt(a, b):
    return lax.dot_general(a, b, (((1,), (1,)), ((), ())), preferred_element_type=F32)


def prep_kernel(tok_ref, cot_ref, out_ref):
    for j in range(2):
        tok_t = tok_ref[:, j * BLK : (j + 1) * BLK].T
        cot = cot_ref[:, j * BLK : (j + 1) * BLK]
        for z in range(NZ):
            out_ref[z, j] = tok_t
            out_ref[z, 2 + j] = cot


def table_kernel(mask_ref, out_ref, cells):
    count = jnp.int32(0)
    for cell in range(ROWS * COLS):
        cells[count] = jnp.int32(cell)
        count = count + mask_ref[cell // COLS, cell % COLS]
    last_row = jnp.int32(-1)
    for s in range(SLOTS):
        used = jnp.int32(s) < count
        cell = jnp.where(used, cells[s], ROWS * COLS - 1)
        row = cell >> 5
        out_ref[s] = cell & 31
        out_ref[SLOTS + s] = row
        out_ref[2 * SLOTS + s] = jnp.where(row == last_row, 0, 1)
        out_ref[3 * SLOTS + s] = jnp.where(used, 1, 0)
        last_row = row


def weights_kernel(up_ref, down_ref, up_t_ref, down_t_ref):
    for s in range(SLOTS):
        up_t_ref[s] = up_ref[s].T
        down_t_ref[s] = down_ref[s].T


def first_kernel(
    table_ref, place_ref, own_ref, other_ref, up_t_ref, down_ref, grads_ref, act_ref, pre_ref, panels, hid, dac
):
    core = place_ref[0]
    panels[0] = own_ref[...]
    panels[1] = other_ref[...]

    def place(s):
        col = table_ref[s]
        return ((col >> 1) & 1) ^ core, col >> 2, col & 1

    hid_sum = jnp.zeros((BLK, BLK), F32)
    dac_sum = jnp.zeros((BLK, BLK), F32)
    for s in range(SLOTS):
        side, z, j = place(s)
        row = table_ref[SLOTS + s]
        fresh = table_ref[2 * SLOTS + s] == 1
        used = table_ref[3 * SLOTS + s] == 1
        hid_part = nn(up_t_ref[s], panels[side, z, j])
        dac_part = nt(down_ref[s], panels[side, z, 2 + j])
        hid_sum = jnp.where(fresh, 0.0, hid_sum) + jnp.where(used, hid_part, 0.0)
        dac_sum = jnp.where(fresh, 0.0, dac_sum) + jnp.where(used, dac_part, 0.0)
        hid[row] = hid_sum
        dac[row] = dac_sum
    for r in range(ROWS):
        act, pre = gelu_pair(hid[r], dac[r])
        act_ref[r] = act
        pre_ref[r] = pre
    for s in range(SLOTS):
        side, z, j = place(s)
        row = table_ref[SLOTS + s]
        used = table_ref[3 * SLOTS + s] == 1
        up_part = nt(panels[side, z, j], pre_ref[row])
        down_part = nn(act_ref[row], panels[side, z, 2 + j])
        grads_ref[s // 8, 0, s % 8] = jnp.where(used, up_part, 0.0).astype(BF)
        grads_ref[s // 8, 1, s % 8] = jnp.where(used, down_part, 0.0).astype(BF)


def second_kernel(table_ref, place_ref, act_ref, pre_ref, down_t_ref, up_ref, own_ref, send_ref, out_sum, grad_sum):
    core = place_ref[0]
    out_sum[...] = jnp.zeros_like(out_sum)
    grad_sum[...] = jnp.zeros_like(grad_sum)
    for s in range(SLOTS):
        col = table_ref[s]
        row = table_ref[SLOTS + s]
        used = table_ref[3 * SLOTS + s] == 1
        out_part = nn(down_t_ref[s], act_ref[row])
        grad_part = nn(up_ref[s], pre_ref[row])
        out_sum[col] += jnp.where(used, out_part, 0.0)
        grad_sum[col] += jnp.where(used, grad_part, 0.0)
    for z in range(NZ):
        for j in range(2):
            own = 4 * z + 2 * core + j
            other = 4 * z + 2 * (1 - core) + j
            own_ref[z, j] = out_sum[own].astype(BF)
            own_ref[z, 2 + j] = grad_sum[own].astype(BF)
            send_ref[z, j] = out_sum[other].astype(BF)
            send_ref[z, 2 + j] = grad_sum[other].astype(BF)


def halve_kernel(level, place_ref, a_ref, b_ref, keep_ref, send_ref):
    bit = (place_ref[1] >> level) & 1
    for half in range(NZ >> (level + 1)):
        near = 2 * half + bit
        far = 2 * half + 1 - bit
        keep_ref[half] = (a_ref[near].astype(F32) + b_ref[near].astype(F32)).astype(BF)
        send_ref[half] = (a_ref[far].astype(F32) + b_ref[far].astype(F32)).astype(BF)


def x_sum_kernel(in_ref, out_ref):
    for y in range(NY):
        for k in range(2):
            total = in_ref[0, k, y].astype(F32)
            for x in range(1, NX):
                total = total + in_ref[x, k, y].astype(F32)
            out_ref[y, k] = total.astype(BF)


def y_sum_kernel(in_ref, out_ref):
    for k in range(2):
        total = in_ref[0, k].astype(F32)
        for y in range(1, NY):
            total = total + in_ref[y, k].astype(F32)
        total = total.astype(BF)
        for y in range(NY):
            out_ref[y, k] = total


def spread_kernel(in_ref, out_ref):
    for y in range(NY):
        for k in range(2):
            tile = in_ref[y, k]
            for x in range(NX):
                out_ref[x, k, y] = tile


def split_kernel(in_ref, up_ref, down_ref):
    for x in range(NX):
        up_ref[x * 8 : (x + 1) * 8] = in_ref[x, 0]
        down_ref[x * 8 : (x + 1) * 8] = in_ref[x, 1]


def final_kernel(a_ref, b_ref, out_ref, grad_ref):
    for j in range(4):
        total = a_ref[0, j].astype(F32) + b_ref[0, j].astype(F32)
        goal = out_ref if j < 2 else grad_ref
        goal[:, (j % 2) * BLK : (j % 2 + 1) * BLK] = total.T.astype(BF)


def whole(count):
    return [pl.BlockSpec(memory_space=pltpu.VMEM)] * count


def smem(count):
    return [pl.BlockSpec(memory_space=pltpu.SMEM)] * count


def shape(*dims, dtype=BF):
    return jax.ShapeDtypeStruct(dims, dtype)


def call(kernel, outs, operands, n_smem=0, scratch=(), flops=0, moved=0, out_smem=False):
    many = isinstance(outs, (list, tuple))
    n_out = len(outs) if many else 1
    out_specs = smem(n_out) if out_smem else whole(n_out)
    return pl.pallas_call(
        kernel,
        out_shape=outs,
        in_specs=smem(n_smem) + whole(len(operands) - n_smem),
        out_specs=out_specs if many else out_specs[0],
        scratch_shapes=list(scratch),
        compiler_params=VM,
        cost_estimate=pl.CostEstimate(flops=flops, bytes_accessed=moved, transcendentals=0),
    )(*operands)


def exchange(x, axis, groups):
    return lax.all_to_all(x, axis, 0, 0, tiled=True, axis_index_groups=groups)


def body(tokens, cotangent, block_mask, up_tiles, down_tiles):
    mib = 1 << 20
    position = lax.axis_index("mp")
    place = jnp.stack([position & 1, position >> 1]).astype(jnp.int32)
    sent = call(prep_kernel, shape(NZ, 4, BLK, BLK), (tokens, cotangent), moved=mib)
    own_panels = exchange(sent, "mp", Z_GROUPS)
    table = call(
        table_kernel,
        shape(4 * SLOTS, dtype=jnp.int32),
        (block_mask,),
        n_smem=1,
        scratch=[pltpu.SMEM((ROWS * COLS + 8,), jnp.int32)],
        out_smem=True,
        flops=mib,
        moved=1024,
    )
    up_t, down_t = call(
        weights_kernel,
        [shape(SLOTS, BLK, BLK), shape(SLOTS, BLK, BLK)],
        (up_tiles, down_tiles),
        moved=4 * mib,
    )
    other_panels = lax.ppermute(own_panels, "mp", CORE_SWAP)
    product = 2 * SLOTS * BLK * BLK * BLK
    grads, act, pre = call(
        first_kernel,
        [shape(NX, 2, 8, BLK, BLK), shape(ROWS, BLK, BLK), shape(ROWS, BLK, BLK)],
        (table, place, own_panels, other_panels, up_t, down_tiles),
        n_smem=2,
        scratch=[
            pltpu.VMEM((2, NZ, 4, BLK, BLK), BF),
            pltpu.VMEM((ROWS, BLK, BLK), F32),
            pltpu.VMEM((ROWS, BLK, BLK), F32),
        ],
        flops=4 * product,
        moved=6 * mib,
    )
    own_part, other_part = call(
        second_kernel,
        [shape(NZ, 4, BLK, BLK), shape(NZ, 4, BLK, BLK)],
        (table, place, act, pre, down_t, up_tiles),
        n_smem=2,
        scratch=[pltpu.VMEM((COLS, BLK, BLK), F32), pltpu.VMEM((COLS, BLK, BLK), F32)],
        flops=2 * product,
        moved=5 * mib,
    )
    from_other = lax.ppermute(other_part, "mp", CORE_SWAP)

    def halve(level, a, b):
        count = NZ >> (level + 1)
        return call(
            functools.partial(halve_kernel, level),
            [shape(count, 4, BLK, BLK)] * 2,
            (place, a, b),
            n_smem=1,
            moved=count * mib // 2,
        )

    keep, send = halve(0, own_part, from_other)
    by_x = exchange(grads, ("dp", "mp"), NEAR_GROUPS)
    by_x, keep, send = lax.optimization_barrier((by_x, keep, send))
    x_done = call(x_sum_kernel, shape(NY, 2, BLK, BLK), (by_x,), moved=3 * mib)
    keep, send = halve(1, keep, lax.ppermute(send, "mp", z_swap(0)))
    by_y = exchange(x_done, ("dp", "mp"), FAR_GROUPS)
    by_y, keep, send = lax.optimization_barrier((by_y, keep, send))
    y_done = call(y_sum_kernel, shape(NY, 2, BLK, BLK), (by_y,), moved=mib)
    keep, send = halve(2, keep, lax.ppermute(send, "mp", z_swap(1)))
    all_y = exchange(y_done, ("dp", "mp"), FAR_GROUPS)
    all_y, keep, send = lax.optimization_barrier((all_y, keep, send))
    spread = call(spread_kernel, shape(NX, 2, NY, BLK, BLK), (all_y,), moved=3 * mib)
    output, grad_tokens = call(
        final_kernel,
        [shape(BLK, 2 * BLK), shape(BLK, 2 * BLK)],
        (keep, lax.ppermute(send, "mp", z_swap(2))),
        moved=mib // 2,
    )
    all_x = exchange(spread, ("dp", "mp"), NEAR_GROUPS)
    grad_up, grad_down = call(
        split_kernel, [shape(SLOTS, BLK, BLK), shape(SLOTS, BLK, BLK)], (all_x,), moved=4 * mib
    )
    return output, grad_tokens, grad_up, grad_down


def solution(mesh):
    in_specs = (
        P("dp", "mp"),
        P("dp", "mp"),
        P("mp", None),
        P("mp", None, None),
        P("mp", None, None),
    )
    out_specs = (P("dp", "mp"), P("dp", "mp"), P("mp", None, None), P("mp", None, None))
    return jax.shard_map(body, mesh=mesh, in_specs=in_specs, out_specs=out_specs, check_vma=False)
```

```python
import functools

import jax
import jax.numpy as jnp
from jax import lax
from jax.experimental import pallas as pl
from jax.experimental.pallas import tpu as pltpu
from jax.sharding import PartitionSpec as P

BF = jnp.bfloat16
F32 = jnp.float32
VM = pltpu.CompilerParams(vmem_limit_bytes=48 * 1024 * 1024)
NX, NY, NZ = 4, 8, 8
N_MP = 2 * NZ


def flat(x, y, mp):
    return ((y % NY) * NX + x % NX) * N_MP + mp


NEAR_GROUPS = [
    [flat(2 * bx + mp % 2 + i, 2 * by + mp % 2 + j, mp) for j in range(2) for i in range(2)]
    for mp in range(N_MP)
    for by in range(NY // 2)
    for bx in range(NX // 2)
]
FAR_GROUPS = [
    [flat(2 * bx + mp % 2 + i, 2 * by + mp % 2 + j, mp) for by in range(NY // 2) for bx in range(NX // 2)]
    for mp in range(N_MP)
    for j in range(2)
    for i in range(2)
]
Z_GROUPS = [[2 * (2 * half + odd) + c for half in range(NZ // 2)] for odd in range(2) for c in range(2)]
CORE_SWAP = [(i, i ^ 1) for i in range(2 * NZ)]


def z_swap(level):
    step = 1 << level
    return [
        (2 * z + c, 2 * ((z + (step if ((z >> level) + c) % 2 == 0 else -step)) % NZ) + c)
        for z in range(NZ)
        for c in range(2)
    ]


SLOTS, ROWS, COLS, BLK = 32, 8, 32, 128


def gelu_pair(hidden, dact):
    inner = 0.7978845608 * (hidden + 0.044715 * hidden * hidden * hidden)
    tangent = jnp.tanh(inner)
    inner_slope = 0.7978845608 * (1.0 + 3.0 * 0.044715 * hidden * hidden)
    value = 0.5 * hidden * (1.0 + tangent)
    slope = 0.5 * (1.0 + tangent) + 0.5 * hidden * (1.0 - tangent * tangent) * inner_slope
    return value.astype(BF), (dact * slope).astype(BF)


def nn(a, b):
    return lax.dot_general(a, b, (((1,), (0,)), ((), ())), preferred_element_type=F32)


def nt(a, b):
    return lax.dot_general(a, b, (((1,), (1,)), ((), ())), preferred_element_type=F32)


def prep_kernel(tok_hbm, cot_hbm, out_ref, tok_ref, cot_ref, sems):
    copies = [
        pltpu.make_async_copy(tok_hbm, tok_ref, sems.at[0]),
        pltpu.make_async_copy(cot_hbm, cot_ref, sems.at[1]),
    ]
    for copy in copies:
        copy.start()
    for copy in copies:
        copy.wait()
    for j in range(2):
        tok_t = tok_ref[:, j * BLK : (j + 1) * BLK].T
        cot = cot_ref[:, j * BLK : (j + 1) * BLK]
        for half in range(NZ // 2):
            out_ref[half, j] = tok_t
            out_ref[half, 2 + j] = cot


def table_kernel(mask_ref, out_ref, cells):
    count = jnp.int32(0)
    for cell in range(ROWS * COLS):
        cells[count] = jnp.int32(cell)
        count = count + mask_ref[cell // COLS, cell % COLS]
    last_row = jnp.int32(-1)
    for s in range(SLOTS):
        used = jnp.int32(s) < count
        cell = jnp.where(used, cells[s], ROWS * COLS - 1)
        row = cell >> 5
        out_ref[s] = cell & 31
        out_ref[SLOTS + s] = row
        out_ref[2 * SLOTS + s] = jnp.where(row == last_row, 0, 1)
        out_ref[3 * SLOTS + s] = jnp.where(used, 1, 0)
        last_row = row


def load_tiles(sources, goals, sems):
    copies = [
        [
            pltpu.make_async_copy(source.at[pl.ds(8 * q, 8)], goal.at[pl.ds(8 * q, 8)], sems.at[q, n])
            for n, (source, goal) in enumerate(zip(sources, goals))
        ]
        for q in range(SLOTS // 8)
    ]
    for group in copies:
        for copy in group:
            copy.start()
    return copies


def wait_tiles(copies, q):
    for copy in copies[q]:
        copy.wait()


def first_kernel(table_ref, place_ref, *refs):
    panel_refs, (up_hbm, down_hbm, grads_hbm, acts_hbm) = refs[:4], refs[4:8]
    panels, hid, dac, grads, acts, up_ref, down_ref, sems, tile_sems = refs[8:]
    loads = load_tiles((up_hbm, down_hbm), (up_ref, down_ref), tile_sems)
    core = place_ref[0]
    odd = place_ref[1] & 1
    for side in range(2):
        for other in range(2):
            panels[side, other] = panel_refs[2 * side + other][...]

    def place(s):
        col = table_ref[s]
        return ((col >> 1) & 1) ^ core, ((col >> 2) & 1) ^ odd, col >> 3, col & 1

    hid_sum = jnp.zeros((BLK, BLK), F32)
    dac_sum = jnp.zeros((BLK, BLK), F32)
    for s in range(SLOTS):
        if s % 8 == 0:
            wait_tiles(loads, s // 8)
        side, other, half, j = place(s)
        row = table_ref[SLOTS + s]
        fresh = table_ref[2 * SLOTS + s] == 1
        used = table_ref[3 * SLOTS + s] == 1
        hid_part = nn(up_ref[s].T, panels[side, other, half, j])
        dac_part = nt(down_ref[s], panels[side, other, half, 2 + j])
        hid_sum = jnp.where(fresh, 0.0, hid_sum) + jnp.where(used, hid_part, 0.0)
        dac_sum = jnp.where(fresh, 0.0, dac_sum) + jnp.where(used, dac_part, 0.0)
        hid[row] = hid_sum
        dac[row] = dac_sum
    for r in range(ROWS):
        act, pre = gelu_pair(hid[r], dac[r])
        acts[0, r] = act
        acts[1, r] = pre
    copies = [pltpu.make_async_copy(acts, acts_hbm, sems.at[4])]
    copies[0].start()
    for s in range(SLOTS):
        side, other, half, j = place(s)
        row = table_ref[SLOTS + s]
        used = table_ref[3 * SLOTS + s] == 1
        up_part = nt(panels[side, other, half, j], acts[1, row])
        down_part = nn(acts[0, row], panels[side, other, half, 2 + j])
        grads[s // 8, 0, s % 8] = jnp.where(used, up_part, 0.0).astype(BF)
        grads[s // 8, 1, s % 8] = jnp.where(used, down_part, 0.0).astype(BF)
        if s % 8 == 7:
            copies.append(pltpu.make_async_copy(grads.at[s // 8], grads_hbm.at[s // 8], sems.at[s // 8]))
            copies[-1].start()
    for copy in copies:
        copy.wait()


def second_kernel(
    table_ref, place_ref, acts_hbm, up_hbm, down_hbm, own_ref, send_ref, *scratch
):
    out_sum, grad_sum, acts_ref, up_ref, down_ref, sem, tile_sems = scratch
    core = place_ref[0]
    copy = pltpu.make_async_copy(acts_hbm, acts_ref, sem)
    copy.start()
    loads = load_tiles((up_hbm, down_hbm), (up_ref, down_ref), tile_sems)
    out_sum[...] = jnp.zeros_like(out_sum)
    grad_sum[...] = jnp.zeros_like(grad_sum)
    copy.wait()
    for s in range(SLOTS):
        if s % 8 == 0:
            wait_tiles(loads, s // 8)
        col = table_ref[s]
        row = table_ref[SLOTS + s]
        used = table_ref[3 * SLOTS + s] == 1
        out_part = nn(down_ref[s].T, acts_ref[0, row])
        grad_part = nn(up_ref[s], acts_ref[1, row])
        out_sum[col] += jnp.where(used, out_part, 0.0)
        grad_sum[col] += jnp.where(used, grad_part, 0.0)
    for z in range(NZ):
        for j in range(2):
            own = 4 * z + 2 * core + j
            other = 4 * z + 2 * (1 - core) + j
            own_ref[z, j] = out_sum[own].astype(BF)
            own_ref[z, 2 + j] = grad_sum[own].astype(BF)
            send_ref[z, j] = out_sum[other].astype(BF)
            send_ref[z, 2 + j] = grad_sum[other].astype(BF)


def halve_kernel(level, place_ref, a_ref, b_ref, keep_ref, send_ref):
    bit = (place_ref[1] >> level) & 1
    for half in range(NZ >> (level + 1)):
        near = 2 * half + bit
        far = 2 * half + 1 - bit
        keep_ref[half] = (a_ref[near].astype(F32) + b_ref[near].astype(F32)).astype(BF)
        send_ref[half] = (a_ref[far].astype(F32) + b_ref[far].astype(F32)).astype(BF)


def x_sum_kernel(in_ref, out_ref):
    for y in range(NY):
        for k in range(2):
            total = in_ref[0, k, y].astype(F32)
            for x in range(1, NX):
                total = total + in_ref[x, k, y].astype(F32)
            out_ref[y, k] = total.astype(BF)


def y_sum_kernel(in_ref, out_ref):
    for k in range(2):
        total = in_ref[0, k].astype(F32)
        for y in range(1, NY):
            total = total + in_ref[y, k].astype(F32)
        total = total.astype(BF)
        for y in range(NY):
            out_ref[y, k] = total


def spread_kernel(in_ref, out_hbm, sems):
    copies = [
        pltpu.make_async_copy(in_ref.at[:, k], out_hbm.at[x, k], sems.at[x, k]) for x in range(NX) for k in range(2)
    ]
    for copy in copies:
        copy.start()
    for copy in copies:
        copy.wait()


def split_kernel(in_ref, up_hbm, down_hbm, sems):
    copies = [
        pltpu.make_async_copy(in_ref.at[x, k], goal.at[pl.ds(x * 8, 8)], sems.at[x, k])
        for x in range(NX)
        for k, goal in enumerate((up_hbm, down_hbm))
    ]
    for copy in copies:
        copy.start()
    for copy in copies:
        copy.wait()


def final_kernel(a_ref, b_ref, out_ref, grad_ref):
    for j in range(4):
        total = a_ref[0, j].astype(F32) + b_ref[0, j].astype(F32)
        goal = out_ref if j < 2 else grad_ref
        goal[:, (j % 2) * BLK : (j % 2 + 1) * BLK] = total.T.astype(BF)


def shape(*dims, dtype=BF):
    return jax.ShapeDtypeStruct(dims, dtype)


def call(kernel, outs, operands, scratch=(), flops=0, moved=0, ins=None, results=None):
    many = isinstance(outs, (list, tuple))
    ins = ins or [pltpu.VMEM] * len(operands)
    results = results or [pltpu.VMEM] * (len(outs) if many else 1)
    out_specs = [pl.BlockSpec(memory_space=space) for space in results]
    return pl.pallas_call(
        kernel,
        out_shape=outs,
        in_specs=[pl.BlockSpec(memory_space=space) for space in ins],
        out_specs=out_specs if many else out_specs[0],
        scratch_shapes=list(scratch),
        compiler_params=VM,
        cost_estimate=pl.CostEstimate(flops=flops, bytes_accessed=moved, transcendentals=0),
    )(*operands)


def exchange(x, axis, groups):
    return lax.all_to_all(x, axis, 0, 0, tiled=True, axis_index_groups=groups)


def body(tokens, cotangent, block_mask, up_tiles, down_tiles):
    mib = 1 << 20
    position = lax.axis_index("mp")
    place = jnp.stack([position & 1, position >> 1]).astype(jnp.int32)
    tokens, cotangent, up_tiles, down_tiles = (
        pltpu.with_memory_space_constraint(x, pltpu.HBM) for x in (tokens, cotangent, up_tiles, down_tiles)
    )
    sent = call(
        prep_kernel,
        shape(NZ // 2, 4, BLK, BLK),
        (tokens, cotangent),
        scratch=[pltpu.VMEM((BLK, 2 * BLK), BF), pltpu.VMEM((BLK, 2 * BLK), BF), pltpu.SemaphoreType.DMA((2,))],
        ins=[pltpu.HBM] * 2,
        moved=mib,
    )
    table = call(
        table_kernel,
        shape(4 * SLOTS, dtype=jnp.int32),
        (block_mask,),
        scratch=[pltpu.SMEM((ROWS * COLS + 8,), jnp.int32)],
        ins=[pltpu.SMEM],
        results=[pltpu.SMEM],
        flops=mib,
        moved=1024,
    )
    same = exchange(sent, "mp", Z_GROUPS)
    other = lax.ppermute(same, "mp", z_swap(0))
    other, table = lax.optimization_barrier((other, table))
    panels = (same, other, lax.ppermute(same, "mp", CORE_SWAP), lax.ppermute(other, "mp", CORE_SWAP))
    product = 2 * SLOTS * BLK * BLK * BLK
    grads, acts = call(
        first_kernel,
        [pltpu.HBM((4, 2, 8, BLK, BLK), BF), pltpu.HBM((2, ROWS, BLK, BLK), BF)],
        (table, place) + panels + (up_tiles, down_tiles),
        scratch=[
            pltpu.VMEM((2, 2, NZ // 2, 4, BLK, BLK), BF),
            pltpu.VMEM((ROWS, BLK, BLK), F32),
            pltpu.VMEM((ROWS, BLK, BLK), F32),
            pltpu.VMEM((4, 2, 8, BLK, BLK), BF),
            pltpu.VMEM((2, ROWS, BLK, BLK), BF),
            pltpu.VMEM((SLOTS, BLK, BLK), BF),
            pltpu.VMEM((SLOTS, BLK, BLK), BF),
            pltpu.SemaphoreType.DMA((5,)),
            pltpu.SemaphoreType.DMA((4, 2)),
        ],
        ins=[pltpu.SMEM] * 2 + [pltpu.VMEM] * 4 + [pltpu.HBM] * 2,
        results=[pltpu.HBM] * 2,
        flops=4 * product,
        moved=6 * mib,
    )
    own_part, other_part = call(
        second_kernel,
        [shape(NZ, 4, BLK, BLK), shape(NZ, 4, BLK, BLK)],
        (table, place, acts, up_tiles, down_tiles),
        scratch=[
            pltpu.VMEM((COLS, BLK, BLK), F32),
            pltpu.VMEM((COLS, BLK, BLK), F32),
            pltpu.VMEM((2, ROWS, BLK, BLK), BF),
            pltpu.VMEM((SLOTS, BLK, BLK), BF),
            pltpu.VMEM((SLOTS, BLK, BLK), BF),
            pltpu.SemaphoreType.DMA,
            pltpu.SemaphoreType.DMA((4, 2)),
        ],
        ins=[pltpu.SMEM] * 2 + [pltpu.HBM] * 3,
        flops=2 * product,
        moved=5 * mib,
    )
    from_other = lax.ppermute(other_part, "mp", CORE_SWAP)

    def halve(level, a, b):
        count = NZ >> (level + 1)
        return call(
            functools.partial(halve_kernel, level),
            [shape(count, 4, BLK, BLK)] * 2,
            (place, a, b),
            ins=[pltpu.SMEM] + [pltpu.VMEM] * 2,
            moved=count * mib // 2,
        )

    keep, send = halve(0, own_part, from_other)
    by_x = exchange(grads, ("dp", "mp"), NEAR_GROUPS)
    by_x, keep, send = lax.optimization_barrier((by_x, keep, send))
    x_done = call(x_sum_kernel, shape(NY, 2, BLK, BLK), (by_x,), moved=3 * mib)
    keep, send = halve(1, keep, lax.ppermute(send, "mp", z_swap(0)))
    by_y = exchange(x_done, ("dp", "mp"), FAR_GROUPS)
    by_y, keep, send = lax.optimization_barrier((by_y, keep, send))
    y_done = call(y_sum_kernel, shape(NY, 2, BLK, BLK), (by_y,), moved=mib)
    keep, send = halve(2, keep, lax.ppermute(send, "mp", z_swap(1)))
    all_y = exchange(y_done, ("dp", "mp"), FAR_GROUPS)
    all_y, keep, send = lax.optimization_barrier((all_y, keep, send))
    eight = [pltpu.SemaphoreType.DMA((NX, 2))]
    spread = call(
        spread_kernel, shape(NX, 2, NY, BLK, BLK), (all_y,), scratch=eight, results=[pltpu.HBM], moved=3 * mib
    )
    output, grad_tokens = call(
        final_kernel,
        [shape(BLK, 2 * BLK), shape(BLK, 2 * BLK)],
        (keep, lax.ppermute(send, "mp", z_swap(2))),
        moved=mib // 2,
    )
    all_x = exchange(spread, ("dp", "mp"), NEAR_GROUPS)
    grad_up, grad_down = call(
        split_kernel,
        [shape(SLOTS, BLK, BLK), shape(SLOTS, BLK, BLK)],
        (all_x,),
        scratch=eight,
        results=[pltpu.HBM] * 2,
        moved=4 * mib,
    )
    return output, grad_tokens, grad_up, grad_down


def solution(mesh):
    in_specs = (
        P("dp", "mp"),
        P("dp", "mp"),
        P("mp", None),
        P("mp", None, None),
        P("mp", None, None),
    )
    out_specs = (P("dp", "mp"), P("dp", "mp"), P("mp", None, None), P("mp", None, None))
    return jax.shard_map(body, mesh=mesh, in_specs=in_specs, out_specs=out_specs, check_vma=False)
```

```python
import functools

import jax
import jax.numpy as jnp
from jax import lax
from jax.experimental import pallas as pl
from jax.experimental.pallas import tpu as pltpu
from jax.sharding import PartitionSpec as P

BF = jnp.bfloat16
F32 = jnp.float32
VM = pltpu.CompilerParams(vmem_limit_bytes=48 * 1024 * 1024)
NX, NY, NZ = 4, 8, 8
N_MP = 2 * NZ


def flat(x, y, mp):
    return ((y % NY) * NX + x % NX) * N_MP + mp


NEAR_GROUPS = [
    [flat(2 * bx + mp % 2 + i, 2 * by + mp % 2 + j, mp) for j in range(2) for i in range(2)]
    for mp in range(N_MP)
    for by in range(NY // 2)
    for bx in range(NX // 2)
]
FAR_GROUPS = [
    [flat(2 * bx + mp % 2 + i, 2 * by + mp % 2 + j, mp) for by in range(NY // 2) for bx in range(NX // 2)]
    for mp in range(N_MP)
    for j in range(2)
    for i in range(2)
]
Z_GROUPS = [[2 * (2 * half + odd) + c for half in range(NZ // 2)] for odd in range(2) for c in range(2)]
CORE_SWAP = [(i, i ^ 1) for i in range(2 * NZ)]


def z_swap(level):
    step = 1 << level
    return [
        (2 * z + c, 2 * ((z + (step if ((z >> level) + c) % 2 == 0 else -step)) % NZ) + c)
        for z in range(NZ)
        for c in range(2)
    ]


SLOTS, ROWS, COLS, BLK = 32, 8, 32, 128


def gelu_pair(hidden, dact):
    inner = 0.7978845608 * (hidden + 0.044715 * hidden * hidden * hidden)
    tangent = jnp.tanh(inner)
    inner_slope = 0.7978845608 * (1.0 + 3.0 * 0.044715 * hidden * hidden)
    value = 0.5 * hidden * (1.0 + tangent)
    slope = 0.5 * (1.0 + tangent) + 0.5 * hidden * (1.0 - tangent * tangent) * inner_slope
    return value.astype(BF), (dact * slope).astype(BF)


def nn(a, b):
    return lax.dot_general(a, b, (((1,), (0,)), ((), ())), preferred_element_type=F32)


def nt(a, b):
    return lax.dot_general(a, b, (((1,), (1,)), ((), ())), preferred_element_type=F32)


def prep_kernel(tok_hbm, cot_hbm, out_ref, tok_ref, cot_ref, sems):
    copies = [
        pltpu.make_async_copy(tok_hbm, tok_ref, sems.at[0]),
        pltpu.make_async_copy(cot_hbm, cot_ref, sems.at[1]),
    ]
    for copy in copies:
        copy.start()
    for copy in copies:
        copy.wait()
    for j in range(2):
        tok_t = tok_ref[:, j * BLK : (j + 1) * BLK].T
        cot = cot_ref[:, j * BLK : (j + 1) * BLK]
        for half in range(NZ // 2):
            out_ref[half, j] = tok_t
            out_ref[half, 2 + j] = cot


def table_kernel(mask_ref, up_hbm, down_hbm, out_ref, up_ref, down_ref, cells, sems):
    copies = [
        pltpu.make_async_copy(up_hbm, up_ref, sems.at[0]),
        pltpu.make_async_copy(down_hbm, down_ref, sems.at[1]),
    ]
    for copy in copies:
        copy.start()
    count = jnp.int32(0)
    for cell in range(ROWS * COLS):
        cells[count] = jnp.int32(cell)
        count = count + mask_ref[cell // COLS, cell % COLS]
    last_row = jnp.int32(-1)
    for s in range(SLOTS):
        used = jnp.int32(s) < count
        cell = jnp.where(used, cells[s], ROWS * COLS - 1)
        row = cell >> 5
        out_ref[s] = cell & 31
        out_ref[SLOTS + s] = row
        out_ref[2 * SLOTS + s] = jnp.where(row == last_row, 0, 1)
        out_ref[3 * SLOTS + s] = jnp.where(used, 1, 0)
        last_row = row
    for copy in copies:
        copy.wait()


def first_kernel(table_ref, place_ref, *refs):
    panel_refs, (up_ref, down_ref, grads_hbm, acts_hbm) = refs[:4], refs[4:8]
    panels, hid, dac, grads, acts, sems, act_sem = refs[8:]
    core = place_ref[0]
    odd = place_ref[1] & 1
    for side in range(2):
        for other in range(2):
            panels[side, other] = panel_refs[2 * side + other][...]

    def place(s):
        col = table_ref[s]
        return ((col >> 1) & 1) ^ core, ((col >> 2) & 1) ^ odd, col >> 3, col & 1

    hid_sum = jnp.zeros((BLK, BLK), F32)
    dac_sum = jnp.zeros((BLK, BLK), F32)
    for s in range(SLOTS):
        side, other, half, j = place(s)
        row = table_ref[SLOTS + s]
        fresh = table_ref[2 * SLOTS + s] == 1
        used = table_ref[3 * SLOTS + s] == 1
        hid_part = nn(up_ref[s].T, panels[side, other, half, j])
        dac_part = nt(down_ref[s], panels[side, other, half, 2 + j])
        hid_sum = jnp.where(fresh, 0.0, hid_sum) + jnp.where(used, hid_part, 0.0)
        dac_sum = jnp.where(fresh, 0.0, dac_sum) + jnp.where(used, dac_part, 0.0)
        hid[row] = hid_sum
        dac[row] = dac_sum
    for r in range(ROWS):
        act, pre = gelu_pair(hid[r], dac[r])
        acts[0, r] = act
        acts[1, r] = pre
    copies = [pltpu.make_async_copy(acts, acts_hbm, act_sem)]
    copies[0].start()
    for s in range(SLOTS):
        side, other, half, j = place(s)
        row = table_ref[SLOTS + s]
        used = table_ref[3 * SLOTS + s] == 1
        up_part = nt(panels[side, other, half, j], acts[1, row])
        down_part = nn(acts[0, row], panels[side, other, half, 2 + j])
        grads[s // 8, 0, s % 8] = jnp.where(used, up_part, 0.0).astype(BF)
        grads[s // 8, 1, s % 8] = jnp.where(used, down_part, 0.0).astype(BF)
        if s % 4 == 3:
            ready = (s // 8, slice(None), pl.ds(s % 8 - 3, 4))
            copies.append(pltpu.make_async_copy(grads.at[ready], grads_hbm.at[ready], sems.at[s // 4]))
            copies[-1].start()
    for copy in copies:
        copy.wait()


def second_kernel(
    table_ref, place_ref, acts_hbm, up_ref, down_ref, own_ref, send_ref, out_sum, grad_sum, acts_ref, sem
):
    core = place_ref[0]
    copy = pltpu.make_async_copy(acts_hbm, acts_ref, sem)
    copy.start()
    out_sum[...] = jnp.zeros_like(out_sum)
    grad_sum[...] = jnp.zeros_like(grad_sum)
    copy.wait()
    for s in range(SLOTS):
        col = table_ref[s]
        row = table_ref[SLOTS + s]
        used = table_ref[3 * SLOTS + s] == 1
        out_part = nn(down_ref[s].T, acts_ref[0, row])
        grad_part = nn(up_ref[s], acts_ref[1, row])
        out_sum[col] += jnp.where(used, out_part, 0.0)
        grad_sum[col] += jnp.where(used, grad_part, 0.0)
    for z in range(NZ):
        for j in range(2):
            own = 4 * z + 2 * core + j
            other = 4 * z + 2 * (1 - core) + j
            own_ref[z, j] = out_sum[own].astype(BF)
            own_ref[z, 2 + j] = grad_sum[own].astype(BF)
            send_ref[z, j] = out_sum[other].astype(BF)
            send_ref[z, 2 + j] = grad_sum[other].astype(BF)


def halve_kernel(level, place_ref, a_ref, b_ref, keep_ref, send_ref):
    bit = (place_ref[1] >> level) & 1
    for half in range(NZ >> (level + 1)):
        near = 2 * half + bit
        far = 2 * half + 1 - bit
        keep_ref[half] = (a_ref[near].astype(F32) + b_ref[near].astype(F32)).astype(BF)
        send_ref[half] = (a_ref[far].astype(F32) + b_ref[far].astype(F32)).astype(BF)


def x_sum_kernel(in_ref, out_ref):
    for y in range(NY):
        for k in range(2):
            total = in_ref[0, k, y].astype(F32)
            for x in range(1, NX):
                total = total + in_ref[x, k, y].astype(F32)
            out_ref[y, k] = total.astype(BF)


def y_sum_kernel(in_ref, out_ref):
    for k in range(2):
        total = in_ref[0, k].astype(F32)
        for y in range(1, NY):
            total = total + in_ref[y, k].astype(F32)
        total = total.astype(BF)
        for y in range(NY):
            out_ref[y, k] = total


def spread_kernel(in_ref, out_hbm, sems):
    copies = [
        pltpu.make_async_copy(in_ref.at[:, k], out_hbm.at[x, k], sems.at[x, k]) for x in range(NX) for k in range(2)
    ]
    for copy in copies:
        copy.start()
    for copy in copies:
        copy.wait()


def split_kernel(in_ref, up_hbm, down_hbm, sems):
    copies = [
        pltpu.make_async_copy(in_ref.at[x, k], goal.at[pl.ds(x * 8, 8)], sems.at[x, k])
        for x in range(NX)
        for k, goal in enumerate((up_hbm, down_hbm))
    ]
    for copy in copies:
        copy.start()
    for copy in copies:
        copy.wait()


def final_kernel(a_ref, b_ref, out_ref, grad_ref):
    for j in range(4):
        total = a_ref[0, j].astype(F32) + b_ref[0, j].astype(F32)
        goal = out_ref if j < 2 else grad_ref
        goal[:, (j % 2) * BLK : (j % 2 + 1) * BLK] = total.T.astype(BF)


def shape(*dims, dtype=BF):
    return jax.ShapeDtypeStruct(dims, dtype)


def call(kernel, outs, operands, scratch=(), flops=0, moved=0, ins=None, results=None):
    many = isinstance(outs, (list, tuple))
    ins = ins or [pltpu.VMEM] * len(operands)
    results = results or [pltpu.VMEM] * (len(outs) if many else 1)
    out_specs = [pl.BlockSpec(memory_space=space) for space in results]
    return pl.pallas_call(
        kernel,
        out_shape=outs,
        in_specs=[pl.BlockSpec(memory_space=space) for space in ins],
        out_specs=out_specs if many else out_specs[0],
        scratch_shapes=list(scratch),
        compiler_params=VM,
        cost_estimate=pl.CostEstimate(flops=flops, bytes_accessed=moved, transcendentals=0),
    )(*operands)


def exchange(x, axis, groups):
    return lax.all_to_all(x, axis, 0, 0, tiled=True, axis_index_groups=groups)


def run_first(table, place, panels, up_tiles, down_tiles):
    return call(
        first_kernel,
        [pltpu.HBM((4, 2, 8, BLK, BLK), BF), pltpu.HBM((2, ROWS, BLK, BLK), BF)],
        (table, place) + panels + (up_tiles, down_tiles),
        scratch=[
            pltpu.VMEM((2, 2, NZ // 2, 4, BLK, BLK), BF),
            pltpu.VMEM((ROWS, BLK, BLK), F32),
            pltpu.VMEM((ROWS, BLK, BLK), F32),
            pltpu.VMEM((4, 2, 8, BLK, BLK), BF),
            pltpu.VMEM((2, ROWS, BLK, BLK), BF),
            pltpu.SemaphoreType.DMA((8,)),
            pltpu.SemaphoreType.DMA,
        ],
        ins=[pltpu.SMEM] * 2 + [pltpu.VMEM] * 6,
        results=[pltpu.HBM] * 2,
        flops=8 * SLOTS * BLK**3,
        moved=6 << 20,
    )


def run_second(table, place, acts, up_tiles, down_tiles):
    return call(
        second_kernel,
        [shape(NZ, 4, BLK, BLK), shape(NZ, 4, BLK, BLK)],
        (table, place, acts, up_tiles, down_tiles),
        scratch=[
            pltpu.VMEM((COLS, BLK, BLK), F32),
            pltpu.VMEM((COLS, BLK, BLK), F32),
            pltpu.VMEM((2, ROWS, BLK, BLK), BF),
            pltpu.SemaphoreType.DMA,
        ],
        ins=[pltpu.SMEM] * 2 + [pltpu.HBM] + [pltpu.VMEM] * 2,
        flops=4 * SLOTS * BLK**3,
        moved=5 << 20,
    )


def body(tokens, cotangent, block_mask, up_tiles, down_tiles):
    mib = 1 << 20
    position = lax.axis_index("mp")
    place = jnp.stack([position & 1, position >> 1]).astype(jnp.int32)
    tokens, cotangent, up_tiles, down_tiles = (
        pltpu.with_memory_space_constraint(x, pltpu.HBM) for x in (tokens, cotangent, up_tiles, down_tiles)
    )
    sent = call(
        prep_kernel,
        shape(NZ // 2, 4, BLK, BLK),
        (tokens, cotangent),
        scratch=[pltpu.VMEM((BLK, 2 * BLK), BF), pltpu.VMEM((BLK, 2 * BLK), BF), pltpu.SemaphoreType.DMA((2,))],
        ins=[pltpu.HBM] * 2,
        moved=mib,
    )
    table, up_tiles, down_tiles = call(
        table_kernel,
        [shape(4 * SLOTS, dtype=jnp.int32), pltpu.VMEM((SLOTS, BLK, BLK), BF), pltpu.VMEM((SLOTS, BLK, BLK), BF)],
        (block_mask, up_tiles, down_tiles),
        scratch=[pltpu.SMEM((ROWS * COLS + 8,), jnp.int32), pltpu.SemaphoreType.DMA((2,))],
        ins=[pltpu.SMEM] + [pltpu.HBM] * 2,
        results=[pltpu.SMEM] + [pltpu.VMEM] * 2,
        flops=mib,
        moved=4 * mib,
    )
    same = exchange(sent, "mp", Z_GROUPS)
    other = lax.ppermute(same, "mp", z_swap(0))
    other, table, up_tiles, down_tiles = lax.optimization_barrier((other, table, up_tiles, down_tiles))
    panels = (same, other, lax.ppermute(same, "mp", CORE_SWAP), lax.ppermute(other, "mp", CORE_SWAP))
    grads, acts = run_first(table, place, panels, up_tiles, down_tiles)
    own_part, other_part = run_second(table, place, acts, up_tiles, down_tiles)
    from_other = lax.ppermute(other_part, "mp", CORE_SWAP)

    def halve(level, a, b):
        count = NZ >> (level + 1)
        return call(
            functools.partial(halve_kernel, level),
            [shape(count, 4, BLK, BLK)] * 2,
            (place, a, b),
            ins=[pltpu.SMEM] + [pltpu.VMEM] * 2,
            moved=count * mib // 2,
        )

    keep, send = halve(0, own_part, from_other)
    by_x = exchange(grads, ("dp", "mp"), NEAR_GROUPS)
    by_x, keep, send = lax.optimization_barrier((by_x, keep, send))
    x_done = call(x_sum_kernel, shape(NY, 2, BLK, BLK), (by_x,), moved=3 * mib)
    keep, send = halve(1, keep, lax.ppermute(send, "mp", z_swap(0)))
    by_y = exchange(x_done, ("dp", "mp"), FAR_GROUPS)
    by_y, keep, send = lax.optimization_barrier((by_y, keep, send))
    y_done = call(y_sum_kernel, shape(NY, 2, BLK, BLK), (by_y,), moved=mib)
    keep, send = halve(2, keep, lax.ppermute(send, "mp", z_swap(1)))
    all_y = exchange(y_done, ("dp", "mp"), FAR_GROUPS)
    all_y, keep, send = lax.optimization_barrier((all_y, keep, send))
    eight = [pltpu.SemaphoreType.DMA((NX, 2))]
    spread = call(
        spread_kernel, shape(NX, 2, NY, BLK, BLK), (all_y,), scratch=eight, results=[pltpu.HBM], moved=3 * mib
    )
    output, grad_tokens = call(
        final_kernel,
        [shape(BLK, 2 * BLK), shape(BLK, 2 * BLK)],
        (keep, lax.ppermute(send, "mp", z_swap(2))),
        moved=mib // 2,
    )
    all_x = exchange(spread, ("dp", "mp"), NEAR_GROUPS)
    grad_up, grad_down = call(
        split_kernel,
        [shape(SLOTS, BLK, BLK), shape(SLOTS, BLK, BLK)],
        (all_x,),
        scratch=eight,
        results=[pltpu.HBM] * 2,
        moved=4 * mib,
    )
    return output, grad_tokens, grad_up, grad_down


def solution(mesh):
    in_specs = (
        P("dp", "mp"),
        P("dp", "mp"),
        P("mp", None),
        P("mp", None, None),
        P("mp", None, None),
    )
    out_specs = (P("dp", "mp"), P("dp", "mp"), P("mp", None, None), P("mp", None, None))
    return jax.shard_map(body, mesh=mesh, in_specs=in_specs, out_specs=out_specs, check_vma=False)
```

```python
import functools

import jax
import jax.numpy as jnp
from jax import lax
from jax.experimental import pallas as pl
from jax.experimental.pallas import tpu as pltpu
from jax.sharding import PartitionSpec as P

BF = jnp.bfloat16
F32 = jnp.float32
VM = pltpu.CompilerParams(vmem_limit_bytes=32 * 1024 * 1024)
NX, NY, NZ = 4, 8, 8
N_MP = 2 * NZ


def flat(x, y, mp):
    return ((y % NY) * NX + x % NX) * N_MP + mp


NEAR_GROUPS = [
    [flat(2 * bx + mp % 2 + i, 2 * by + mp % 2 + j, mp) for j in range(2) for i in range(2)]
    for mp in range(N_MP)
    for by in range(NY // 2)
    for bx in range(NX // 2)
]
FAR_GROUPS = [
    [flat(2 * bx + mp % 2 + i, 2 * by + mp % 2 + j, mp) for by in range(NY // 2) for bx in range(NX // 2)]
    for mp in range(N_MP)
    for j in range(2)
    for i in range(2)
]
Z_GROUPS = [[2 * (2 * half + odd) + c for half in range(NZ // 2)] for odd in range(2) for c in range(2)]
CORE_SWAP = [(i, i ^ 1) for i in range(2 * NZ)]


def z_swap(level):
    step = 1 << level
    return [
        (2 * z + c, 2 * ((z + (step if ((z >> level) + c) % 2 == 0 else -step)) % NZ) + c)
        for z in range(NZ)
        for c in range(2)
    ]


SLOTS, ROWS, COLS, BLK = 32, 8, 32, 128


def gelu_pair(hidden, dact):
    inner = 0.7978845608 * (hidden + 0.044715 * hidden * hidden * hidden)
    tangent = jnp.tanh(inner)
    inner_slope = 0.7978845608 * (1.0 + 3.0 * 0.044715 * hidden * hidden)
    value = 0.5 * hidden * (1.0 + tangent)
    slope = 0.5 * (1.0 + tangent) + 0.5 * hidden * (1.0 - tangent * tangent) * inner_slope
    return value.astype(BF), (dact * slope).astype(BF)


def nn(a, b):
    return lax.dot_general(a, b, (((1,), (0,)), ((), ())), preferred_element_type=F32)


def nt(a, b):
    return lax.dot_general(a, b, (((1,), (1,)), ((), ())), preferred_element_type=F32)


def prep_kernel(tok_hbm, cot_hbm, out_ref, tok_ref, cot_ref, sems):
    copies = [
        pltpu.make_async_copy(tok_hbm, tok_ref, sems.at[0]),
        pltpu.make_async_copy(cot_hbm, cot_ref, sems.at[1]),
    ]
    for copy in copies:
        copy.start()
    for copy in copies:
        copy.wait()
    for j in range(2):
        tok_t = tok_ref[:, j * BLK : (j + 1) * BLK].T
        cot = cot_ref[:, j * BLK : (j + 1) * BLK]
        for half in range(NZ // 2):
            out_ref[half, j] = tok_t
            out_ref[half, 2 + j] = cot


def table_kernel(mask_ref, up_hbm, down_hbm, out_ref, up_ref, down_ref, cells, sems):
    copies = [
        pltpu.make_async_copy(up_hbm, up_ref, sems.at[0]),
        pltpu.make_async_copy(down_hbm, down_ref, sems.at[1]),
    ]
    for copy in copies:
        copy.start()
    count = jnp.int32(0)
    for cell in range(ROWS * COLS):
        cells[count] = jnp.int32(cell)
        count = count + mask_ref[cell // COLS, cell % COLS]
    last_row = jnp.int32(-1)
    for s in range(SLOTS):
        used = jnp.int32(s) < count
        cell = jnp.where(used, cells[s], ROWS * COLS - 1)
        row = cell >> 5
        out_ref[s] = cell & 31
        out_ref[SLOTS + s] = row
        out_ref[2 * SLOTS + s] = jnp.where(row == last_row, 0, 1)
        out_ref[3 * SLOTS + s] = jnp.where(used, 1, 0)
        last_row = row
    for copy in copies:
        copy.wait()


def first_kernel(table_ref, place_ref, *refs):
    panel_refs, (up_ref, down_ref, grads_hbm, acts_hbm) = refs[:4], refs[4:8]
    panels, hid, dac, grads, acts, sems, act_sem = refs[8:]
    core = place_ref[0]
    odd = place_ref[1] & 1
    for side in range(2):
        for other in range(2):
            panels[side, other] = panel_refs[2 * side + other][...]

    def place(s):
        col = table_ref[s]
        return ((col >> 1) & 1) ^ core, ((col >> 2) & 1) ^ odd, col >> 3, col & 1

    hid_sum = jnp.zeros((BLK, BLK), F32)
    dac_sum = jnp.zeros((BLK, BLK), F32)
    for s in range(SLOTS):
        side, other, half, j = place(s)
        row = table_ref[SLOTS + s]
        fresh = table_ref[2 * SLOTS + s] == 1
        used = table_ref[3 * SLOTS + s] == 1
        hid_part = nn(up_ref[s].T, panels[side, other, half, j])
        dac_part = nt(down_ref[s], panels[side, other, half, 2 + j])
        hid_sum = jnp.where(fresh, 0.0, hid_sum) + jnp.where(used, hid_part, 0.0)
        dac_sum = jnp.where(fresh, 0.0, dac_sum) + jnp.where(used, dac_part, 0.0)
        hid[row] = hid_sum
        dac[row] = dac_sum
    for r in range(ROWS):
        act, pre = gelu_pair(hid[r], dac[r])
        acts[0, r] = act
        acts[1, r] = pre
    copies = [pltpu.make_async_copy(acts, acts_hbm, act_sem)]
    copies[0].start()
    for s in range(SLOTS):
        side, other, half, j = place(s)
        row = table_ref[SLOTS + s]
        used = table_ref[3 * SLOTS + s] == 1
        up_part = nt(panels[side, other, half, j], acts[1, row])
        down_part = nn(acts[0, row], panels[side, other, half, 2 + j])
        grads[s // 8, 0, s % 8] = jnp.where(used, up_part, 0.0).astype(BF)
        grads[s // 8, 1, s % 8] = jnp.where(used, down_part, 0.0).astype(BF)
        if s % 4 == 3:
            ready = (s // 8, slice(None), pl.ds(s % 8 - 3, 4))
            copies.append(pltpu.make_async_copy(grads.at[ready], grads_hbm.at[ready], sems.at[s // 4]))
            copies[-1].start()
    for copy in copies:
        copy.wait()


def second_kernel(
    table_ref, place_ref, acts_hbm, up_ref, down_ref, own_ref, send_ref, out_sum, grad_sum, acts_ref, sem
):
    core = place_ref[0]
    copy = pltpu.make_async_copy(acts_hbm, acts_ref, sem)
    copy.start()
    out_sum[...] = jnp.zeros_like(out_sum)
    grad_sum[...] = jnp.zeros_like(grad_sum)
    copy.wait()
    for s in range(SLOTS):
        col = table_ref[s]
        row = table_ref[SLOTS + s]
        used = table_ref[3 * SLOTS + s] == 1
        out_part = nn(down_ref[s].T, acts_ref[0, row])
        grad_part = nn(up_ref[s], acts_ref[1, row])
        out_sum[col] += jnp.where(used, out_part, 0.0)
        grad_sum[col] += jnp.where(used, grad_part, 0.0)
    for z in range(NZ):
        for j in range(2):
            own = 4 * z + 2 * core + j
            other = 4 * z + 2 * (1 - core) + j
            own_ref[z, j] = out_sum[own].astype(BF)
            own_ref[z, 2 + j] = grad_sum[own].astype(BF)
            send_ref[z, j] = out_sum[other].astype(BF)
            send_ref[z, 2 + j] = grad_sum[other].astype(BF)


def halve_kernel(level, place_ref, a_ref, b_ref, keep_ref, send_ref):
    bit = (place_ref[1] >> level) & 1
    for half in range(NZ >> (level + 1)):
        near = 2 * half + bit
        far = 2 * half + 1 - bit
        keep_ref[half] = (a_ref[near].astype(F32) + b_ref[near].astype(F32)).astype(BF)
        send_ref[half] = (a_ref[far].astype(F32) + b_ref[far].astype(F32)).astype(BF)


def x_sum_kernel(in_ref, out_hbm, sums, sems):
    copies = []
    for y in range(NY):
        for k in range(2):
            total = in_ref[0, k, y].astype(F32)
            for x in range(1, NX):
                total = total + in_ref[x, k, y].astype(F32)
            sums[y, k] = total.astype(BF)
        copies.append(pltpu.make_async_copy(sums.at[y], out_hbm.at[y], sems.at[y]))
        copies[-1].start()
    for copy in copies:
        copy.wait()


def y_sum_kernel(in_ref, out_hbm, sums, sems):
    for k in range(2):
        total = in_ref[0, k].astype(F32)
        for y in range(1, NY):
            total = total + in_ref[y, k].astype(F32)
        sums[k] = total.astype(BF)
    copies = [pltpu.make_async_copy(sums, out_hbm.at[y], sems.at[y]) for y in range(NY)]
    for copy in copies:
        copy.start()
    for copy in copies:
        copy.wait()


def spread_kernel(in_ref, out_hbm, sems):
    copies = [
        pltpu.make_async_copy(in_ref.at[:, k], out_hbm.at[x, k], sems.at[x, k]) for x in range(NX) for k in range(2)
    ]
    for copy in copies:
        copy.start()
    for copy in copies:
        copy.wait()


def split_kernel(in_ref, up_hbm, down_hbm, sems):
    copies = [
        pltpu.make_async_copy(in_ref.at[x, k], goal.at[pl.ds(x * 8, 8)], sems.at[x, k])
        for x in range(NX)
        for k, goal in enumerate((up_hbm, down_hbm))
    ]
    for copy in copies:
        copy.start()
    for copy in copies:
        copy.wait()


def final_kernel(a_ref, b_ref, out_ref, grad_ref):
    for j in range(4):
        total = a_ref[0, j].astype(F32) + b_ref[0, j].astype(F32)
        goal = out_ref if j < 2 else grad_ref
        goal[:, (j % 2) * BLK : (j % 2 + 1) * BLK] = total.T.astype(BF)


def shape(*dims, dtype=BF):
    return jax.ShapeDtypeStruct(dims, dtype)


def call(kernel, outs, operands, scratch=(), flops=0, moved=0, ins=None, results=None):
    many = isinstance(outs, (list, tuple))
    ins = ins or [pltpu.VMEM] * len(operands)
    results = results or [pltpu.VMEM] * (len(outs) if many else 1)
    out_specs = [pl.BlockSpec(memory_space=space) for space in results]
    return pl.pallas_call(
        kernel,
        out_shape=outs,
        in_specs=[pl.BlockSpec(memory_space=space) for space in ins],
        out_specs=out_specs if many else out_specs[0],
        scratch_shapes=list(scratch),
        compiler_params=VM,
        cost_estimate=pl.CostEstimate(flops=flops, bytes_accessed=moved, transcendentals=0),
    )(*operands)


def exchange(x, axis, groups):
    return lax.all_to_all(x, axis, 0, 0, tiled=True, axis_index_groups=groups)


def run_first(table, place, panels, up_tiles, down_tiles):
    return call(
        first_kernel,
        [pltpu.HBM((4, 2, 8, BLK, BLK), BF), pltpu.HBM((2, ROWS, BLK, BLK), BF)],
        (table, place) + panels + (up_tiles, down_tiles),
        scratch=[
            pltpu.VMEM((2, 2, NZ // 2, 4, BLK, BLK), BF),
            pltpu.VMEM((ROWS, BLK, BLK), F32),
            pltpu.VMEM((ROWS, BLK, BLK), F32),
            pltpu.VMEM((4, 2, 8, BLK, BLK), BF),
            pltpu.VMEM((2, ROWS, BLK, BLK), BF),
            pltpu.SemaphoreType.DMA((8,)),
            pltpu.SemaphoreType.DMA,
        ],
        ins=[pltpu.SMEM] * 2 + [pltpu.VMEM] * 6,
        results=[pltpu.HBM] * 2,
        flops=8 * SLOTS * BLK**3,
        moved=6 << 20,
    )


def run_second(table, place, acts, up_tiles, down_tiles):
    return call(
        second_kernel,
        [shape(NZ, 4, BLK, BLK), shape(NZ, 4, BLK, BLK)],
        (table, place, acts, up_tiles, down_tiles),
        scratch=[
            pltpu.VMEM((COLS, BLK, BLK), F32),
            pltpu.VMEM((COLS, BLK, BLK), F32),
            pltpu.VMEM((2, ROWS, BLK, BLK), BF),
            pltpu.SemaphoreType.DMA,
        ],
        ins=[pltpu.SMEM] * 2 + [pltpu.HBM] + [pltpu.VMEM] * 2,
        flops=4 * SLOTS * BLK**3,
        moved=5 << 20,
    )


def body(tokens, cotangent, block_mask, up_tiles, down_tiles):
    mib = 1 << 20
    position = lax.axis_index("mp")
    place = jnp.stack([position & 1, position >> 1]).astype(jnp.int32)
    tokens, cotangent, up_tiles, down_tiles = (
        pltpu.with_memory_space_constraint(x, pltpu.HBM) for x in (tokens, cotangent, up_tiles, down_tiles)
    )
    sent = call(
        prep_kernel,
        shape(NZ // 2, 4, BLK, BLK),
        (tokens, cotangent),
        scratch=[pltpu.VMEM((BLK, 2 * BLK), BF), pltpu.VMEM((BLK, 2 * BLK), BF), pltpu.SemaphoreType.DMA((2,))],
        ins=[pltpu.HBM] * 2,
        moved=mib,
    )
    table, up_tiles, down_tiles = call(
        table_kernel,
        [shape(4 * SLOTS, dtype=jnp.int32), pltpu.VMEM((SLOTS, BLK, BLK), BF), pltpu.VMEM((SLOTS, BLK, BLK), BF)],
        (block_mask, up_tiles, down_tiles),
        scratch=[pltpu.SMEM((ROWS * COLS + 8,), jnp.int32), pltpu.SemaphoreType.DMA((2,))],
        ins=[pltpu.SMEM] + [pltpu.HBM] * 2,
        results=[pltpu.SMEM] + [pltpu.VMEM] * 2,
        flops=mib,
        moved=4 * mib,
    )
    same = exchange(sent, "mp", Z_GROUPS)
    other = lax.ppermute(same, "mp", z_swap(0))
    other, table, up_tiles, down_tiles = lax.optimization_barrier((other, table, up_tiles, down_tiles))
    panels = (same, other, lax.ppermute(same, "mp", CORE_SWAP), lax.ppermute(other, "mp", CORE_SWAP))
    grads, acts = run_first(table, place, panels, up_tiles, down_tiles)
    own_part, other_part = run_second(table, place, acts, up_tiles, down_tiles)
    from_other = lax.ppermute(other_part, "mp", CORE_SWAP)

    def halve(level, a, b):
        count = NZ >> (level + 1)
        return call(
            functools.partial(halve_kernel, level),
            [shape(count, 4, BLK, BLK)] * 2,
            (place, a, b),
            ins=[pltpu.SMEM] + [pltpu.VMEM] * 2,
            moved=count * mib // 2,
        )

    keep, send = halve(0, own_part, from_other)
    by_x = exchange(grads, ("dp", "mp"), NEAR_GROUPS)
    by_x, keep, send = lax.optimization_barrier((by_x, keep, send))
    x_done = call(
        x_sum_kernel,
        pltpu.HBM((NY, 2, BLK, BLK), BF),
        (by_x,),
        scratch=[pltpu.VMEM((NY, 2, BLK, BLK), BF), pltpu.SemaphoreType.DMA((NY,))],
        results=[pltpu.HBM],
        moved=3 * mib,
    )
    keep, send = halve(1, keep, lax.ppermute(send, "mp", z_swap(0)))
    by_y = exchange(x_done, ("dp", "mp"), FAR_GROUPS)
    by_y, keep, send = lax.optimization_barrier((by_y, keep, send))
    y_done = call(
        y_sum_kernel,
        pltpu.HBM((NY, 2, BLK, BLK), BF),
        (by_y,),
        scratch=[pltpu.VMEM((2, BLK, BLK), BF), pltpu.SemaphoreType.DMA((NY,))],
        results=[pltpu.HBM],
        moved=mib,
    )
    keep, send = halve(2, keep, lax.ppermute(send, "mp", z_swap(1)))
    all_y = exchange(y_done, ("dp", "mp"), FAR_GROUPS)
    all_y, keep, send = lax.optimization_barrier((all_y, keep, send))
    eight = [pltpu.SemaphoreType.DMA((NX, 2))]
    spread = call(
        spread_kernel, shape(NX, 2, NY, BLK, BLK), (all_y,), scratch=eight, results=[pltpu.HBM], moved=3 * mib
    )
    output, grad_tokens = call(
        final_kernel,
        [shape(BLK, 2 * BLK), shape(BLK, 2 * BLK)],
        (keep, lax.ppermute(send, "mp", z_swap(2))),
        moved=mib // 2,
    )
    all_x = exchange(spread, ("dp", "mp"), NEAR_GROUPS)
    grad_up, grad_down = call(
        split_kernel,
        [shape(SLOTS, BLK, BLK), shape(SLOTS, BLK, BLK)],
        (all_x,),
        scratch=eight,
        results=[pltpu.HBM] * 2,
        moved=4 * mib,
    )
    return output, grad_tokens, grad_up, grad_down


def solution(mesh):
    in_specs = (
        P("dp", "mp"),
        P("dp", "mp"),
        P("mp", None),
        P("mp", None, None),
        P("mp", None, None),
    )
    out_specs = (P("dp", "mp"), P("dp", "mp"), P("mp", None, None), P("mp", None, None))
    return jax.shard_map(body, mesh=mesh, in_specs=in_specs, out_specs=out_specs, check_vma=False)
```

```python
import functools

import jax
import jax.numpy as jnp
from jax import lax
from jax.experimental import pallas as pl
from jax.experimental.pallas import tpu as pltpu
from jax.sharding import PartitionSpec as P

BF = jnp.bfloat16
F32 = jnp.float32
VM = pltpu.CompilerParams(vmem_limit_bytes=32 * 1024 * 1024)
NX, NY, NZ = 4, 8, 8
N_MP = 2 * NZ


def flat(x, y, mp):
    return ((y % NY) * NX + x % NX) * N_MP + mp


NEAR_GROUPS = [
    [flat(2 * bx + mp % 2 + i, 2 * by + mp % 2 + j, mp) for j in range(2) for i in range(2)]
    for mp in range(N_MP)
    for by in range(NY // 2)
    for bx in range(NX // 2)
]
FAR_GROUPS = [
    [flat(2 * bx + mp % 2 + i, 2 * by + mp % 2 + j, mp) for by in range(NY // 2) for bx in range(NX // 2)]
    for mp in range(N_MP)
    for j in range(2)
    for i in range(2)
]
Z_GROUPS = [[2 * (2 * half + odd) + c for half in (0, 2, 1, 3)] for odd in range(2) for c in range(2)]
CORE_SWAP = [(i, i ^ 1) for i in range(2 * NZ)]


def z_swap(level):
    step = 1 << level
    return [
        (2 * z + c, 2 * ((z + (step if ((z >> level) + c) % 2 == 0 else -step)) % NZ) + c)
        for z in range(NZ)
        for c in range(2)
    ]


SLOTS, ROWS, COLS, BLK = 32, 8, 32, 128


def gelu_pair(hidden, dact):
    inner = 0.7978845608 * (hidden + 0.044715 * hidden * hidden * hidden)
    tangent = jnp.tanh(inner)
    inner_slope = 0.7978845608 * (1.0 + 3.0 * 0.044715 * hidden * hidden)
    value = 0.5 * hidden * (1.0 + tangent)
    slope = 0.5 * (1.0 + tangent) + 0.5 * hidden * (1.0 - tangent * tangent) * inner_slope
    return value.astype(BF), (dact * slope).astype(BF)


def nn(a, b):
    return lax.dot_general(a, b, (((1,), (0,)), ((), ())), preferred_element_type=F32)


def nt(a, b):
    return lax.dot_general(a, b, (((1,), (1,)), ((), ())), preferred_element_type=F32)


def prep_kernel(tok_hbm, cot_hbm, out_ref, tok_ref, cot_ref, sems):
    copies = [
        pltpu.make_async_copy(tok_hbm, tok_ref, sems.at[0]),
        pltpu.make_async_copy(cot_hbm, cot_ref, sems.at[1]),
    ]
    for copy in copies:
        copy.start()
    for copy in copies:
        copy.wait()
    for j in range(2):
        tok_t = tok_ref[:, j * BLK : (j + 1) * BLK].T
        cot = cot_ref[:, j * BLK : (j + 1) * BLK]
        for half in range(NZ // 2):
            out_ref[half, j] = tok_t
            out_ref[half, 2 + j] = cot


def table_kernel(mask_ref, up_hbm, down_hbm, out_ref, up_ref, down_ref, cells, sems):
    copies = [
        pltpu.make_async_copy(up_hbm, up_ref, sems.at[0]),
        pltpu.make_async_copy(down_hbm, down_ref, sems.at[1]),
    ]
    for copy in copies:
        copy.start()
    count = jnp.int32(0)
    for cell in range(ROWS * COLS):
        cells[count] = jnp.int32(cell)
        count = count + mask_ref[cell // COLS, cell % COLS]
    last_row = jnp.int32(-1)
    for s in range(SLOTS):
        used = jnp.int32(s) < count
        cell = jnp.where(used, cells[s], ROWS * COLS - 1)
        row = cell >> 5
        out_ref[s] = cell & 31
        out_ref[SLOTS + s] = row
        out_ref[2 * SLOTS + s] = jnp.where(row == last_row, 0, 1)
        out_ref[3 * SLOTS + s] = jnp.where(used, 1, 0)
        last_row = row
    for copy in copies:
        copy.wait()


def first_kernel(table_ref, place_ref, *refs):
    panel_refs, (up_ref, down_ref, grads_hbm, acts_hbm) = refs[:4], refs[4:8]
    panels, hid, dac, grads, acts, sems, act_sem = refs[8:]
    core = place_ref[0]
    odd = place_ref[1] & 1
    for side in range(2):
        for other in range(2):
            panels[side, other] = panel_refs[2 * side + other][...]

    def place(s):
        col = table_ref[s]
        half = 2 * ((col >> 3) & 1) + (col >> 4)
        return ((col >> 1) & 1) ^ core, ((col >> 2) & 1) ^ odd, half, col & 1

    hid_sum = jnp.zeros((BLK, BLK), F32)
    dac_sum = jnp.zeros((BLK, BLK), F32)
    for s in range(SLOTS):
        side, other, half, j = place(s)
        row = table_ref[SLOTS + s]
        fresh = table_ref[2 * SLOTS + s] == 1
        used = table_ref[3 * SLOTS + s] == 1
        hid_part = nn(up_ref[s].T, panels[side, other, half, j])
        dac_part = nt(down_ref[s], panels[side, other, half, 2 + j])
        hid_sum = jnp.where(fresh, 0.0, hid_sum) + jnp.where(used, hid_part, 0.0)
        dac_sum = jnp.where(fresh, 0.0, dac_sum) + jnp.where(used, dac_part, 0.0)
        hid[row] = hid_sum
        dac[row] = dac_sum
    for r in range(ROWS):
        act, pre = gelu_pair(hid[r], dac[r])
        acts[0, r] = act
        acts[1, r] = pre
    copies = [pltpu.make_async_copy(acts, acts_hbm, act_sem)]
    copies[0].start()
    for s in range(SLOTS):
        side, other, half, j = place(s)
        row = table_ref[SLOTS + s]
        used = table_ref[3 * SLOTS + s] == 1
        up_part = nt(panels[side, other, half, j], acts[1, row])
        down_part = nn(acts[0, row], panels[side, other, half, 2 + j])
        grads[s // 8, 0, s % 8] = jnp.where(used, up_part, 0.0).astype(BF)
        grads[s // 8, 1, s % 8] = jnp.where(used, down_part, 0.0).astype(BF)
        if s % 4 == 3:
            ready = (s // 8, slice(None), pl.ds(s % 8 - 3, 4))
            copies.append(pltpu.make_async_copy(grads.at[ready], grads_hbm.at[ready], sems.at[s // 4]))
            copies[-1].start()
    for copy in copies:
        copy.wait()


def second_kernel(
    table_ref, place_ref, acts_hbm, up_ref, down_ref, own_ref, send_ref, out_sum, grad_sum, acts_ref, sem
):
    core = place_ref[0]
    copy = pltpu.make_async_copy(acts_hbm, acts_ref, sem)
    copy.start()
    out_sum[...] = jnp.zeros_like(out_sum)
    grad_sum[...] = jnp.zeros_like(grad_sum)
    copy.wait()
    for s in range(SLOTS):
        col = table_ref[s]
        row = table_ref[SLOTS + s]
        used = table_ref[3 * SLOTS + s] == 1
        out_part = nn(down_ref[s].T, acts_ref[0, row])
        grad_part = nn(up_ref[s], acts_ref[1, row])
        out_sum[col] += jnp.where(used, out_part, 0.0)
        grad_sum[col] += jnp.where(used, grad_part, 0.0)
    for z in range(NZ):
        for j in range(2):
            own = 4 * z + 2 * core + j
            other = 4 * z + 2 * (1 - core) + j
            own_ref[z, j] = out_sum[own].astype(BF)
            own_ref[z, 2 + j] = grad_sum[own].astype(BF)
            send_ref[z, j] = out_sum[other].astype(BF)
            send_ref[z, 2 + j] = grad_sum[other].astype(BF)


def halve_kernel(level, place_ref, a_ref, b_ref, keep_ref, send_ref):
    bit = (place_ref[1] >> level) & 1
    for half in range(NZ >> (level + 1)):
        near = 2 * half + bit
        far = 2 * half + 1 - bit
        keep_ref[half] = (a_ref[near].astype(F32) + b_ref[near].astype(F32)).astype(BF)
        send_ref[half] = (a_ref[far].astype(F32) + b_ref[far].astype(F32)).astype(BF)


def x_sum_kernel(in_ref, out_hbm, sums, sems):
    copies = []
    for y in range(NY):
        for k in range(2):
            total = in_ref[0, k, y].astype(F32)
            for x in range(1, NX):
                total = total + in_ref[x, k, y].astype(F32)
            sums[y, k] = total.astype(BF)
        copies.append(pltpu.make_async_copy(sums.at[y], out_hbm.at[y], sems.at[y]))
        copies[-1].start()
    for copy in copies:
        copy.wait()


def y_sum_kernel(in_ref, out_hbm, sums, sems):
    for k in range(2):
        total = in_ref[0, k].astype(F32)
        for y in range(1, NY):
            total = total + in_ref[y, k].astype(F32)
        sums[k] = total.astype(BF)
    copies = [pltpu.make_async_copy(sums, out_hbm.at[y], sems.at[y]) for y in range(NY)]
    for copy in copies:
        copy.start()
    for copy in copies:
        copy.wait()


def spread_kernel(in_ref, out_hbm, sems):
    copies = [
        pltpu.make_async_copy(in_ref.at[:, k], out_hbm.at[x, k], sems.at[x, k]) for x in range(NX) for k in range(2)
    ]
    for copy in copies:
        copy.start()
    for copy in copies:
        copy.wait()


def split_kernel(in_ref, up_hbm, down_hbm, sems):
    copies = [
        pltpu.make_async_copy(in_ref.at[x, k], goal.at[pl.ds(x * 8, 8)], sems.at[x, k])
        for x in range(NX)
        for k, goal in enumerate((up_hbm, down_hbm))
    ]
    for copy in copies:
        copy.start()
    for copy in copies:
        copy.wait()


def final_kernel(a_ref, b_ref, out_ref, grad_ref):
    for j in range(4):
        total = a_ref[0, j].astype(F32) + b_ref[0, j].astype(F32)
        goal = out_ref if j < 2 else grad_ref
        goal[:, (j % 2) * BLK : (j % 2 + 1) * BLK] = total.T.astype(BF)


def shape(*dims, dtype=BF):
    return jax.ShapeDtypeStruct(dims, dtype)


def call(kernel, outs, operands, scratch=(), flops=0, moved=0, ins=None, results=None):
    many = isinstance(outs, (list, tuple))
    ins = ins or [pltpu.VMEM] * len(operands)
    results = results or [pltpu.VMEM] * (len(outs) if many else 1)
    out_specs = [pl.BlockSpec(memory_space=space) for space in results]
    return pl.pallas_call(
        kernel,
        out_shape=outs,
        in_specs=[pl.BlockSpec(memory_space=space) for space in ins],
        out_specs=out_specs if many else out_specs[0],
        scratch_shapes=list(scratch),
        compiler_params=VM,
        cost_estimate=pl.CostEstimate(flops=flops, bytes_accessed=moved, transcendentals=0),
    )(*operands)


def exchange(x, axis, groups):
    return lax.all_to_all(x, axis, 0, 0, tiled=True, axis_index_groups=groups)


def run_first(table, place, panels, up_tiles, down_tiles):
    return call(
        first_kernel,
        [pltpu.HBM((4, 2, 8, BLK, BLK), BF), pltpu.HBM((2, ROWS, BLK, BLK), BF)],
        (table, place) + panels + (up_tiles, down_tiles),
        scratch=[
            pltpu.VMEM((2, 2, NZ // 2, 4, BLK, BLK), BF),
            pltpu.VMEM((ROWS, BLK, BLK), F32),
            pltpu.VMEM((ROWS, BLK, BLK), F32),
            pltpu.VMEM((4, 2, 8, BLK, BLK), BF),
            pltpu.VMEM((2, ROWS, BLK, BLK), BF),
            pltpu.SemaphoreType.DMA((8,)),
            pltpu.SemaphoreType.DMA,
        ],
        ins=[pltpu.SMEM] * 2 + [pltpu.VMEM] * 6,
        results=[pltpu.HBM] * 2,
        flops=8 * SLOTS * BLK**3,
        moved=6 << 20,
    )


def run_second(table, place, acts, up_tiles, down_tiles):
    return call(
        second_kernel,
        [shape(NZ, 4, BLK, BLK), shape(NZ, 4, BLK, BLK)],
        (table, place, acts, up_tiles, down_tiles),
        scratch=[
            pltpu.VMEM((COLS, BLK, BLK), F32),
            pltpu.VMEM((COLS, BLK, BLK), F32),
            pltpu.VMEM((2, ROWS, BLK, BLK), BF),
            pltpu.SemaphoreType.DMA,
        ],
        ins=[pltpu.SMEM] * 2 + [pltpu.HBM] + [pltpu.VMEM] * 2,
        flops=4 * SLOTS * BLK**3,
        moved=5 << 20,
    )


def body(tokens, cotangent, block_mask, up_tiles, down_tiles):
    mib = 1 << 20
    position = lax.axis_index("mp")
    place = jnp.stack([position & 1, position >> 1]).astype(jnp.int32)
    tokens, cotangent, up_tiles, down_tiles = (
        pltpu.with_memory_space_constraint(x, pltpu.HBM) for x in (tokens, cotangent, up_tiles, down_tiles)
    )
    sent = call(
        prep_kernel,
        shape(NZ // 2, 4, BLK, BLK),
        (tokens, cotangent),
        scratch=[pltpu.VMEM((BLK, 2 * BLK), BF), pltpu.VMEM((BLK, 2 * BLK), BF), pltpu.SemaphoreType.DMA((2,))],
        ins=[pltpu.HBM] * 2,
        moved=mib,
    )
    table, up_tiles, down_tiles = call(
        table_kernel,
        [shape(4 * SLOTS, dtype=jnp.int32), pltpu.VMEM((SLOTS, BLK, BLK), BF), pltpu.VMEM((SLOTS, BLK, BLK), BF)],
        (block_mask, up_tiles, down_tiles),
        scratch=[pltpu.SMEM((ROWS * COLS + 8,), jnp.int32), pltpu.SemaphoreType.DMA((2,))],
        ins=[pltpu.SMEM] + [pltpu.HBM] * 2,
        results=[pltpu.SMEM] + [pltpu.VMEM] * 2,
        flops=mib,
        moved=4 * mib,
    )
    same = exchange(sent, "mp", Z_GROUPS)
    other = lax.ppermute(same, "mp", z_swap(0))
    other, table, up_tiles, down_tiles = lax.optimization_barrier((other, table, up_tiles, down_tiles))
    panels = (same, other, lax.ppermute(same, "mp", CORE_SWAP), lax.ppermute(other, "mp", CORE_SWAP))
    grads, acts = run_first(table, place, panels, up_tiles, down_tiles)
    own_part, other_part = run_second(table, place, acts, up_tiles, down_tiles)
    from_other = lax.ppermute(other_part, "mp", CORE_SWAP)

    def halve(level, a, b):
        count = NZ >> (level + 1)
        return call(
            functools.partial(halve_kernel, level),
            [shape(count, 4, BLK, BLK)] * 2,
            (place, a, b),
            ins=[pltpu.SMEM] + [pltpu.VMEM] * 2,
            moved=count * mib // 2,
        )

    keep, send = halve(0, own_part, from_other)
    by_x = exchange(grads, ("dp", "mp"), NEAR_GROUPS)
    by_x, keep, send = lax.optimization_barrier((by_x, keep, send))
    x_done = call(
        x_sum_kernel,
        pltpu.HBM((NY, 2, BLK, BLK), BF),
        (by_x,),
        scratch=[pltpu.VMEM((NY, 2, BLK, BLK), BF), pltpu.SemaphoreType.DMA((NY,))],
        results=[pltpu.HBM],
        moved=3 * mib,
    )
    keep, send = halve(1, keep, lax.ppermute(send, "mp", z_swap(0)))
    by_y = exchange(x_done, ("dp", "mp"), FAR_GROUPS)
    by_y, keep, send = lax.optimization_barrier((by_y, keep, send))
    y_done = call(
        y_sum_kernel,
        pltpu.HBM((NY, 2, BLK, BLK), BF),
        (by_y,),
        scratch=[pltpu.VMEM((2, BLK, BLK), BF), pltpu.SemaphoreType.DMA((NY,))],
        results=[pltpu.HBM],
        moved=mib,
    )
    keep, send = halve(2, keep, lax.ppermute(send, "mp", z_swap(1)))
    all_y = exchange(y_done, ("dp", "mp"), FAR_GROUPS)
    all_y, keep, send = lax.optimization_barrier((all_y, keep, send))
    eight = [pltpu.SemaphoreType.DMA((NX, 2))]
    spread = call(
        spread_kernel, shape(NX, 2, NY, BLK, BLK), (all_y,), scratch=eight, results=[pltpu.HBM], moved=3 * mib
    )
    output, grad_tokens = call(
        final_kernel,
        [shape(BLK, 2 * BLK), shape(BLK, 2 * BLK)],
        (keep, lax.ppermute(send, "mp", z_swap(2))),
        moved=mib // 2,
    )
    all_x = exchange(spread, ("dp", "mp"), NEAR_GROUPS)
    grad_up, grad_down = call(
        split_kernel,
        [shape(SLOTS, BLK, BLK), shape(SLOTS, BLK, BLK)],
        (all_x,),
        scratch=eight,
        results=[pltpu.HBM] * 2,
        moved=4 * mib,
    )
    return output, grad_tokens, grad_up, grad_down


def solution(mesh):
    in_specs = (
        P("dp", "mp"),
        P("dp", "mp"),
        P("mp", None),
        P("mp", None, None),
        P("mp", None, None),
    )
    out_specs = (P("dp", "mp"), P("dp", "mp"), P("mp", None, None), P("mp", None, None))
    return jax.shard_map(body, mesh=mesh, in_specs=in_specs, out_specs=out_specs, check_vma=False)
```

```python
import functools

import jax
import jax.numpy as jnp
from jax import lax
from jax.experimental import pallas as pl
from jax.experimental.pallas import tpu as pltpu
from jax.sharding import PartitionSpec as P

BF = jnp.bfloat16
F32 = jnp.float32
VM = pltpu.CompilerParams(vmem_limit_bytes=48 * 1024 * 1024)
NX, NY, NZ = 4, 8, 8
N_MP = 2 * NZ


def flat(x, y, mp):
    return ((y % NY) * NX + x % NX) * N_MP + mp


NEAR_GROUPS = [
    [flat(2 * bx + mp % 2 + i, 2 * by + mp % 2 + j, mp) for j in range(2) for i in range(2)]
    for mp in range(N_MP)
    for by in range(NY // 2)
    for bx in range(NX // 2)
]
FAR_GROUPS = [
    [flat(2 * bx + mp % 2 + i, 2 * by + mp % 2 + j, mp) for by in range(NY // 2) for bx in range(NX // 2)]
    for mp in range(N_MP)
    for j in range(2)
    for i in range(2)
]
Z_GROUPS = [[2 * (2 * half + odd) + c for half in range(NZ // 2)] for odd in range(2) for c in range(2)]
CORE_SWAP = [(i, i ^ 1) for i in range(2 * NZ)]


def z_swap(level):
    step = 1 << level
    return [
        (2 * z + c, 2 * ((z + (step if ((z >> level) + c) % 2 == 0 else -step)) % NZ) + c)
        for z in range(NZ)
        for c in range(2)
    ]


SLOTS, ROWS, COLS, BLK = 32, 8, 32, 128


def gelu_pair(hidden, dact):
    inner = 0.7978845608 * (hidden + 0.044715 * hidden * hidden * hidden)
    tangent = jnp.tanh(inner)
    inner_slope = 0.7978845608 * (1.0 + 3.0 * 0.044715 * hidden * hidden)
    value = 0.5 * hidden * (1.0 + tangent)
    slope = 0.5 * (1.0 + tangent) + 0.5 * hidden * (1.0 - tangent * tangent) * inner_slope
    return value.astype(BF), (dact * slope).astype(BF)


def nn(a, b):
    return lax.dot_general(a, b, (((1,), (0,)), ((), ())), preferred_element_type=F32)


def nt(a, b):
    return lax.dot_general(a, b, (((1,), (1,)), ((), ())), preferred_element_type=F32)


def prep_kernel(tok_hbm, cot_hbm, out_ref, tok_ref, cot_ref, sems):
    copies = [
        pltpu.make_async_copy(tok_hbm, tok_ref, sems.at[0]),
        pltpu.make_async_copy(cot_hbm, cot_ref, sems.at[1]),
    ]
    for copy in copies:
        copy.start()
    for copy in copies:
        copy.wait()
    for j in range(2):
        tok_t = tok_ref[:, j * BLK : (j + 1) * BLK].T
        cot = cot_ref[:, j * BLK : (j + 1) * BLK]
        for half in range(NZ // 2):
            out_ref[half, j] = tok_t
            out_ref[half, 2 + j] = cot


def table_kernel(mask_ref, up_hbm, down_hbm, out_ref, up_ref, down_ref, cells, sems):
    copies = [
        pltpu.make_async_copy(up_hbm, up_ref, sems.at[0]),
        pltpu.make_async_copy(down_hbm, down_ref, sems.at[1]),
    ]
    for copy in copies:
        copy.start()
    count = jnp.int32(0)
    for cell in range(ROWS * COLS):
        cells[count] = jnp.int32(cell)
        count = count + mask_ref[cell // COLS, cell % COLS]
    last_row = jnp.int32(-1)
    for s in range(SLOTS):
        used = jnp.int32(s) < count
        cell = jnp.where(used, cells[s], ROWS * COLS - 1)
        row = cell >> 5
        out_ref[s] = cell & 31
        out_ref[SLOTS + s] = row
        out_ref[2 * SLOTS + s] = jnp.where(row == last_row, 0, 1)
        out_ref[3 * SLOTS + s] = jnp.where(used, 1, 0)
        last_row = row
    for copy in copies:
        copy.wait()


def first_kernel(table_ref, place_ref, *refs):
    panel_refs, (up_ref, down_ref, grads_hbm, acts_hbm) = refs[:4], refs[4:8]
    panels, hid, dac, grads, acts, sems, act_sem = refs[8:]
    core = place_ref[0]
    odd = place_ref[1] & 1
    for side in range(2):
        for other in range(2):
            panels[side, other] = panel_refs[2 * side + other][...]

    def place(s):
        col = table_ref[s]
        return ((col >> 1) & 1) ^ core, ((col >> 2) & 1) ^ odd, col >> 3, col & 1

    hid_sum = jnp.zeros((BLK, BLK), F32)
    dac_sum = jnp.zeros((BLK, BLK), F32)
    for s in range(SLOTS):
        side, other, half, j = place(s)
        row = table_ref[SLOTS + s]
        fresh = table_ref[2 * SLOTS + s] == 1
        used = table_ref[3 * SLOTS + s] == 1
        hid_part = nn(up_ref[s].T, panels[side, other, half, j])
        dac_part = nt(down_ref[s], panels[side, other, half, 2 + j])
        hid_sum = jnp.where(fresh, 0.0, hid_sum) + jnp.where(used, hid_part, 0.0)
        dac_sum = jnp.where(fresh, 0.0, dac_sum) + jnp.where(used, dac_part, 0.0)
        hid[row] = hid_sum
        dac[row] = dac_sum
    for r in range(ROWS):
        act, pre = gelu_pair(hid[r], dac[r])
        acts[0, r] = act
        acts[1, r] = pre
    copies = [pltpu.make_async_copy(acts, acts_hbm, act_sem)]
    copies[0].start()
    for s in range(SLOTS):
        side, other, half, j = place(s)
        row = table_ref[SLOTS + s]
        used = table_ref[3 * SLOTS + s] == 1
        up_part = nt(panels[side, other, half, j], acts[1, row])
        down_part = nn(acts[0, row], panels[side, other, half, 2 + j])
        grads[s // 8, 0, s % 8] = jnp.where(used, up_part, 0.0).astype(BF)
        grads[s // 8, 1, s % 8] = jnp.where(used, down_part, 0.0).astype(BF)
        if s % 8 == 7:
            copies.append(pltpu.make_async_copy(grads.at[s // 8], grads_hbm.at[s // 8], sems.at[s // 8]))
            copies[-1].start()
    for copy in copies:
        copy.wait()


def second_kernel(
    table_ref, place_ref, acts_hbm, up_ref, down_ref, own_ref, send_ref, out_sum, grad_sum, acts_ref, sem
):
    core = place_ref[0]
    copy = pltpu.make_async_copy(acts_hbm, acts_ref, sem)
    copy.start()
    out_sum[...] = jnp.zeros_like(out_sum)
    grad_sum[...] = jnp.zeros_like(grad_sum)
    copy.wait()
    for s in range(SLOTS):
        col = table_ref[s]
        row = table_ref[SLOTS + s]
        used = table_ref[3 * SLOTS + s] == 1
        out_part = nn(down_ref[s].T, acts_ref[0, row])
        grad_part = nn(up_ref[s], acts_ref[1, row])
        out_sum[col] += jnp.where(used, out_part, 0.0)
        grad_sum[col] += jnp.where(used, grad_part, 0.0)
    for z in range(NZ):
        for j in range(2):
            own = 4 * z + 2 * core + j
            other = 4 * z + 2 * (1 - core) + j
            own_ref[z, j] = out_sum[own].astype(BF)
            own_ref[z, 2 + j] = grad_sum[own].astype(BF)
            send_ref[z, j] = out_sum[other].astype(BF)
            send_ref[z, 2 + j] = grad_sum[other].astype(BF)


def halve_kernel(level, place_ref, a_ref, b_ref, keep_ref, send_ref):
    bit = (place_ref[1] >> level) & 1
    for half in range(NZ >> (level + 1)):
        near = 2 * half + bit
        far = 2 * half + 1 - bit
        keep_ref[half] = (a_ref[near].astype(F32) + b_ref[near].astype(F32)).astype(BF)
        send_ref[half] = (a_ref[far].astype(F32) + b_ref[far].astype(F32)).astype(BF)


def x_sum_kernel(in_ref, out_ref):
    for y in range(NY):
        for k in range(2):
            total = in_ref[0, k, y].astype(F32)
            for x in range(1, NX):
                total = total + in_ref[x, k, y].astype(F32)
            out_ref[y, k] = total.astype(BF)


def y_sum_kernel(in_ref, out_ref):
    for k in range(2):
        total = in_ref[0, k].astype(F32)
        for y in range(1, NY):
            total = total + in_ref[y, k].astype(F32)
        total = total.astype(BF)
        for y in range(NY):
            out_ref[y, k] = total


def spread_kernel(in_ref, out_hbm, sems):
    copies = [
        pltpu.make_async_copy(in_ref.at[:, k], out_hbm.at[x, k], sems.at[x, k]) for x in range(NX) for k in range(2)
    ]
    for copy in copies:
        copy.start()
    for copy in copies:
        copy.wait()


def split_kernel(in_ref, up_hbm, down_hbm, sems):
    copies = [
        pltpu.make_async_copy(in_ref.at[x, k], goal.at[pl.ds(x * 8, 8)], sems.at[x, k])
        for x in range(NX)
        for k, goal in enumerate((up_hbm, down_hbm))
    ]
    for copy in copies:
        copy.start()
    for copy in copies:
        copy.wait()


def final_kernel(a_ref, b_ref, out_ref, grad_ref):
    for j in range(4):
        total = a_ref[0, j].astype(F32) + b_ref[0, j].astype(F32)
        goal = out_ref if j < 2 else grad_ref
        goal[:, (j % 2) * BLK : (j % 2 + 1) * BLK] = total.T.astype(BF)


def shape(*dims, dtype=BF):
    return jax.ShapeDtypeStruct(dims, dtype)


def call(kernel, outs, operands, scratch=(), flops=0, moved=0, ins=None, results=None):
    many = isinstance(outs, (list, tuple))
    ins = ins or [pltpu.VMEM] * len(operands)
    results = results or [pltpu.VMEM] * (len(outs) if many else 1)
    out_specs = [pl.BlockSpec(memory_space=space) for space in results]
    return pl.pallas_call(
        kernel,
        out_shape=outs,
        in_specs=[pl.BlockSpec(memory_space=space) for space in ins],
        out_specs=out_specs if many else out_specs[0],
        scratch_shapes=list(scratch),
        compiler_params=VM,
        cost_estimate=pl.CostEstimate(flops=flops, bytes_accessed=moved, transcendentals=0),
    )(*operands)


def exchange(x, axis, groups):
    return lax.all_to_all(x, axis, 0, 0, tiled=True, axis_index_groups=groups)


def run_first(table, place, panels, up_tiles, down_tiles):
    return call(
        first_kernel,
        [pltpu.HBM((4, 2, 8, BLK, BLK), BF), pltpu.HBM((2, ROWS, BLK, BLK), BF)],
        (table, place) + panels + (up_tiles, down_tiles),
        scratch=[
            pltpu.VMEM((2, 2, NZ // 2, 4, BLK, BLK), BF),
            pltpu.VMEM((ROWS, BLK, BLK), F32),
            pltpu.VMEM((ROWS, BLK, BLK), F32),
            pltpu.VMEM((4, 2, 8, BLK, BLK), BF),
            pltpu.VMEM((2, ROWS, BLK, BLK), BF),
            pltpu.SemaphoreType.DMA((4,)),
            pltpu.SemaphoreType.DMA,
        ],
        ins=[pltpu.SMEM] * 2 + [pltpu.VMEM] * 6,
        results=[pltpu.HBM] * 2,
        flops=8 * SLOTS * BLK**3,
        moved=6 << 20,
    )


def run_second(table, place, acts, up_tiles, down_tiles):
    return call(
        second_kernel,
        [shape(NZ, 4, BLK, BLK), shape(NZ, 4, BLK, BLK)],
        (table, place, acts, up_tiles, down_tiles),
        scratch=[
            pltpu.VMEM((COLS, BLK, BLK), F32),
            pltpu.VMEM((COLS, BLK, BLK), F32),
            pltpu.VMEM((2, ROWS, BLK, BLK), BF),
            pltpu.SemaphoreType.DMA,
        ],
        ins=[pltpu.SMEM] * 2 + [pltpu.HBM] + [pltpu.VMEM] * 2,
        flops=4 * SLOTS * BLK**3,
        moved=5 << 20,
    )


def body(tokens, cotangent, block_mask, up_tiles, down_tiles):
    mib = 1 << 20
    position = lax.axis_index("mp")
    place = jnp.stack([position & 1, position >> 1]).astype(jnp.int32)
    tokens, cotangent, up_tiles, down_tiles = (
        pltpu.with_memory_space_constraint(x, pltpu.HBM) for x in (tokens, cotangent, up_tiles, down_tiles)
    )
    sent = call(
        prep_kernel,
        shape(NZ // 2, 4, BLK, BLK),
        (tokens, cotangent),
        scratch=[pltpu.VMEM((BLK, 2 * BLK), BF), pltpu.VMEM((BLK, 2 * BLK), BF), pltpu.SemaphoreType.DMA((2,))],
        ins=[pltpu.HBM] * 2,
        moved=mib,
    )
    table, up_tiles, down_tiles = call(
        table_kernel,
        [shape(4 * SLOTS, dtype=jnp.int32), pltpu.VMEM((SLOTS, BLK, BLK), BF), pltpu.VMEM((SLOTS, BLK, BLK), BF)],
        (block_mask, up_tiles, down_tiles),
        scratch=[pltpu.SMEM((ROWS * COLS + 8,), jnp.int32), pltpu.SemaphoreType.DMA((2,))],
        ins=[pltpu.SMEM] + [pltpu.HBM] * 2,
        results=[pltpu.SMEM] + [pltpu.VMEM] * 2,
        flops=mib,
        moved=4 * mib,
    )
    same = exchange(sent, "mp", Z_GROUPS)
    other = lax.ppermute(same, "mp", z_swap(0))
    other, table, up_tiles, down_tiles = lax.optimization_barrier((other, table, up_tiles, down_tiles))
    panels = (same, other, lax.ppermute(same, "mp", CORE_SWAP), lax.ppermute(other, "mp", CORE_SWAP))
    grads, acts = run_first(table, place, panels, up_tiles, down_tiles)
    own_part, other_part = run_second(table, place, acts, up_tiles, down_tiles)
    from_other = lax.ppermute(other_part, "mp", CORE_SWAP)

    def halve(level, a, b):
        count = NZ >> (level + 1)
        return call(
            functools.partial(halve_kernel, level),
            [shape(count, 4, BLK, BLK)] * 2,
            (place, a, b),
            ins=[pltpu.SMEM] + [pltpu.VMEM] * 2,
            moved=count * mib // 2,
        )

    keep, send = halve(0, own_part, from_other)
    by_x = exchange(grads, ("dp", "mp"), NEAR_GROUPS)
    by_x, keep, send = lax.optimization_barrier((by_x, keep, send))
    x_done = call(x_sum_kernel, shape(NY, 2, BLK, BLK), (by_x,), moved=3 * mib)
    keep, send = halve(1, keep, lax.ppermute(send, "mp", z_swap(0)))
    by_y = exchange(x_done, ("dp", "mp"), FAR_GROUPS)
    by_y, keep, send = lax.optimization_barrier((by_y, keep, send))
    y_done = call(y_sum_kernel, shape(NY, 2, BLK, BLK), (by_y,), moved=mib)
    keep, send = halve(2, keep, lax.ppermute(send, "mp", z_swap(1)))
    all_y = exchange(y_done, ("dp", "mp"), FAR_GROUPS)
    all_y, keep, send = lax.optimization_barrier((all_y, keep, send))
    eight = [pltpu.SemaphoreType.DMA((NX, 2))]
    spread = call(
        spread_kernel, shape(NX, 2, NY, BLK, BLK), (all_y,), scratch=eight, results=[pltpu.HBM], moved=3 * mib
    )
    output, grad_tokens = call(
        final_kernel,
        [shape(BLK, 2 * BLK), shape(BLK, 2 * BLK)],
        (keep, lax.ppermute(send, "mp", z_swap(2))),
        moved=mib // 2,
    )
    all_x = exchange(spread, ("dp", "mp"), NEAR_GROUPS)
    grad_up, grad_down = call(
        split_kernel,
        [shape(SLOTS, BLK, BLK), shape(SLOTS, BLK, BLK)],
        (all_x,),
        scratch=eight,
        results=[pltpu.HBM] * 2,
        moved=4 * mib,
    )
    return output, grad_tokens, grad_up, grad_down


def solution(mesh):
    in_specs = (
        P("dp", "mp"),
        P("dp", "mp"),
        P("mp", None),
        P("mp", None, None),
        P("mp", None, None),
    )
    out_specs = (P("dp", "mp"), P("dp", "mp"), P("mp", None, None), P("mp", None, None))
    return jax.shard_map(body, mesh=mesh, in_specs=in_specs, out_specs=out_specs, check_vma=False)
```
